128 devices in a mesh: cells: 32 (over x, z, core), holes: 4 (over y).
Axes of the slice: x: 4, y: 4, z: 4, core: 2. Of those that a mesh axis runs over, the one named last changes fastest.
Arguments:
- pole_grads: bfloat16 [6144, 3, 8192], P('holes', None, 'cells'), may hold values from -3 to 3
- endpoints: int32 [4096, 2], P('holes'), may hold values from 0 to 6143
- current: int32 [16384], P('holes'), may hold values from 0 to 1023
- potential: int32 [16384], P('holes'), may hold values from 0 to 4095
- live_counts: int32 [4], replicated, may hold values from 1 to 4096, 10240 in all
- cell_weight: float32 [8192], P('cells'), may hold values from 0.3 to 3
- basis: bfloat16 [8192, 256], P('cells'), may hold values from -0.125 to 0.125
Outputs:
- gains: bfloat16 [256, 16384], P('cells', 'holes')
The draws below stay inside these ranges and needn't reach their ends.
All inputs are finite; a program needn't handle non-finite values.
Results may differ from the reference program's by a relative error of at most 0.011.
Values may be sent and summed in bfloat16 or wider, within the bound.
A program may use at most 128 MiB of HBM per device.

```python
import math
import jax
import jax.numpy as jnp
import numpy as np
from jax import lax

POLES = 6144
BASIS = 256
DIP_G = 1024
Q_G = 4096
CELLS = 8192
GROUPS = 4
DIPOLES = 4096
CANDIDATES = 16384


def place_ends(entries, key, low, largest):
    place = [jax.random.randint(jax.random.fold_in(key, axis), (), 0, length) for axis, length in enumerate(entries.shape)]
    main_axis = entries.shape.index(max(entries.shape))
    beside = place[:main_axis] + [(place[main_axis] + 1) % entries.shape[main_axis]] + place[main_axis + 1:]
    return entries.at[tuple(place)].set(low).at[tuple(beside)].set(largest)


def spiked(result, rng, source, target, blocks, factor):
    def block_of(dim):
        return (jnp.arange(result.shape[dim]) // (result.shape[dim] // blocks)).reshape((-1,) + (1,) * (result.ndim - 1 - dim))

    first = jax.random.permutation(rng, blocks)[block_of(target)]
    second = (block_of(target) + blocks // 2) % blocks
    return jnp.where((block_of(source) == first) | (block_of(source) == second), factor * result, result)


def shard_levels(rng, extent, cuts, smallest, top_value):
    loudness = 1.0
    for dim, blocks in cuts:
        draws = jax.random.uniform(jax.random.fold_in(jax.random.fold_in(rng, 6), dim), (blocks,), jnp.float32, smallest / len(cuts), top_value / len(cuts))
        loudness = loudness * jnp.repeat(jnp.exp(draws), extent[dim] // blocks).reshape((-1,) + (1,) * (len(extent) - 1 - dim))
    return loudness


def split_up(count, total, reach, lean):
    portions = [(1 << 20) // math.isqrt(rank ** lean) + 1 for rank in range(2, count + 1)]
    surplus, holding = total - reach - (count - 1), [1] * (count - 1)
    while surplus > 0:
        movable = [i for i in range(count - 1) if holding[i] < reach]
        pool, left = sum([portions[i] for i in movable]), surplus
        for i in movable:
            addition = min(reach - holding[i], max(1, left * portions[i] // pool), surplus)
            holding[i] = holding[i] + addition
            surplus = surplus - addition
    return np.array([reach] + holding)


def uneven_parts(rng, amount, total, most, skew):
    if amount == 2:
        one = jax.random.randint(rng, (), max(1, total - most), min(most, total - 1) + 1)
        return jnp.stack([one, total - one])
    tallies = jnp.asarray(split_up(amount, total, most, skew), jnp.int32)
    couples = (amount - 1) // 2
    source_of, receiver = tallies[1:1 + 2 * couples:2], tallies[2:2 + 2 * couples:2]
    margin = jnp.minimum(source_of - 1, most - receiver)
    moved = jax.random.randint(jax.random.fold_in(rng, 1), (couples,), 0, 1 << 20) % (margin + 1)
    tallies = tallies.at[1:1 + 2 * couples:2].set(source_of - moved).at[2:2 + 2 * couples:2].set(receiver + moved)
    return tallies[jax.random.permutation(jax.random.fold_in(rng, 2), amount)]


def bell_draw(own_key, extent, width, most, cuts=(), kind=jnp.bfloat16):
    result = jax.random.normal(own_key, extent, jnp.float32) * width
    if len(cuts) > 0:
        result = shard_levels(own_key, extent, cuts, -0.22, 0.18) * result
    return jnp.clip(result, min=-most, max=most).astype(kind)


def noise_with(own_key, shape, scale, limit, split, heavy, kind=jnp.bfloat16):
    drawn = scale * jax.random.normal(own_key, shape, jnp.float32)
    if split:
        drawn = drawn * shard_levels(own_key, shape, split, -0.22, 0.18)
    return jnp.clip(spiked(drawn, jax.random.fold_in(own_key, 3), *heavy), -limit, limit).astype(kind)


def setup_inputs(seed: int = 0) -> dict:
    arg_keys = jax.random.split(jax.random.key(seed), 8)
    pole_grads = bell_draw(arg_keys[0], (POLES, 3, CELLS), 0.5, 3.0, ((0, 4), (2, 32)))
    endpoints = place_ends(jax.random.randint(arg_keys[1], (DIPOLES, 2), 0, POLES), jax.random.fold_in(arg_keys[1], 1), 0, POLES - 1).astype(jnp.int32)
    current = place_ends(jax.random.randint(arg_keys[2], (CANDIDATES,), 0, DIP_G), jax.random.fold_in(arg_keys[2], 1), 0, DIP_G - 1).astype(jnp.int32)
    potential = place_ends(jax.random.randint(arg_keys[3], (CANDIDATES,), 0, DIPOLES), jax.random.fold_in(arg_keys[3], 1), 0, DIPOLES - 1).astype(jnp.int32)
    live_counts = uneven_parts(arg_keys[4], GROUPS, GROUPS * Q_G * 5 // 8, Q_G, 2).astype(jnp.int32)
    cell_weight = jnp.clip(jnp.exp(math.log(3.0) - 2.3025851 * jax.random.uniform(arg_keys[5], (CELLS,), jnp.float32) ** shard_levels(arg_keys[5], (CELLS,), ((0, 32),), -0.2, 0.2)), 0.3, 3.0)
    basis = noise_with(arg_keys[6], (CELLS, BASIS), CELLS ** -0.5, 0.125, ((0, 32),), (0, 1, 32, 2.75))
    return {"pole_grads": pole_grads, "endpoints": endpoints, "current": current, "potential": potential, "live_counts": live_counts, "cell_weight": cell_weight, "basis": basis}


def reference(pole_grads, endpoints, current, potential, live_counts, cell_weight, basis):
    plus = jnp.take(pole_grads, endpoints[:, 0], axis=0).astype(jnp.float32)
    minus = jnp.take(pole_grads, endpoints[:, 1], axis=0).astype(jnp.float32)
    fields = (plus - minus).astype(jnp.bfloat16)
    block = min(512, Q_G)
    blocks = CANDIDATES // block

    def one_block(index):
        rows = index * block + lax.iota(jnp.int32, block)
        group = rows // Q_G
        near = jnp.take(fields, group * DIP_G + jnp.take(current, rows), axis=0).astype(jnp.float32)
        far = jnp.take(fields, jnp.take(potential, rows), axis=0).astype(jnp.float32)
        sens = (jnp.sum(near * far, axis=1) * cell_weight[None, :]).astype(jnp.bfloat16)
        proj = lax.dot_general(basis, sens, (((0,), (1,)), ((), ())), preferred_element_type=jnp.float32)
        alive = (rows - group * Q_G) < jnp.take(live_counts, group)
        return jnp.where(alive[None, :], proj, jnp.float32(0.0))

    parts = lax.map(one_block, jnp.arange(blocks, dtype=jnp.int32))
    return jnp.transpose(parts, (1, 0, 2)).reshape(BASIS, CANDIDATES).astype(jnp.bfloat16)
```

```python
import functools

import jax
import jax.numpy as jnp
from jax import lax
from jax.experimental import pallas as pl
from jax.experimental.pallas import tpu as pltpu
from jax.sharding import PartitionSpec as P

F32, BF16, I32 = jnp.float32, jnp.bfloat16, jnp.int32
MESH = pl.DeviceIdType.MESH

LANES = 128
NY, NX, NZ, CORES = 4, 4, 4, 2
CHIPS = NX * NZ
POLES_G, DIP_G, Q_G, BASIS = 1536, 1024, 4096, 256
PARTS = 4
PIECE = POLES_G // PARTS
ROW = 4
BLOCK = 128
OWN_BLOCKS = 11
OWN_Q = OWN_BLOCKS * BLOCK
SUBS = ((0, 4), (4, 8), (8, 11))
ALL_Q = NY * CORES * OWN_Q
IDX_ROWS = 80


def first_blocks(live):
    starts = [0]
    for g in range(NY - 1):
        starts.append(starts[-1] + (live(g) + (BLOCK - 1)) // BLOCK)
    return starts


def kernel(poles, endp, cur, pot, block_rows, weight, basis, out,
           landed, ptab, dtab, own_idx, all_idx, idx, prod, sent, came, wts, bas, bas_t, part, got,
           pole_send, pole_recv, fwd_send, fwd_recv, own_sem, idx_send, idx_recv, idx_sem,
           small_send, small_recv, sens_send, sens_recv, part_send, part_recv, out_send, out_recv):
    cells, y = lax.axis_index("cells"), lax.axis_index("holes")
    core, chip = lax.rem(cells, CORES), lax.div(cells, CORES)
    x, z = lax.div(chip, NZ), lax.rem(chip, NZ)
    sibling = (chip * CORES + 1 - core, y)

    def on_ring(dy):
        return lax.rem(y + dy, NY)

    def on_plane(dx, dz):
        return lax.rem(x + dx, NX) * NZ + lax.rem(z + dz, NZ)

    deltas = [(dx, dz) for dx in range(NX) for dz in range(NZ) if dx or dz]
    back = [deltas.index(((NX - dx) % NX, (NZ - dz) % NZ)) for dx, dz in deltas]

    barrier = pltpu.get_barrier_semaphore()
    for dc in range(CORES):
        for dy in range(NY):
            if dc or dy:
                pl.semaphore_signal(barrier, inc=1, device_id=(chip * CORES + lax.rem(core + dc, CORES), on_ring(dy)), device_id_type=MESH)
    for dx, dz in deltas:
        pl.semaphore_signal(barrier, inc=1, device_id=(on_plane(dx, dz) * CORES + core, y), device_id_type=MESH)

    own_idx[0:16, :] = endp[...] * ROW
    own_idx[16:48, :] = (cur[...] + y * DIP_G) * ROW
    own_idx[48:80, :] = pot[...] * ROW
    wts[core] = weight[...]
    for h in range(2):
        bas[core * 2 + h] = basis[h * LANES:(h + 1) * LANES, :]

    pl.semaphore_wait(barrier, NY * CORES - 1 + len(deltas))

    idx_copies = []
    for dy in range(1, NY):
        idx_copies.append(pltpu.make_async_remote_copy(
            src_ref=own_idx, dst_ref=all_idx.at[pl.ds(pl.multiple_of(y * IDX_ROWS, 8), IDX_ROWS), :], send_sem=idx_send.at[dy], recv_sem=idx_recv.at[dy],
            device_id=(cells, on_ring(dy)), device_id_type=MESH))
        idx_copies[-1].start()
    all_idx[pl.ds(pl.multiple_of(y * IDX_ROWS, 8), IDX_ROWS), :] = own_idx[...]

    def rows_of(group, piece):
        return pl.ds(pl.multiple_of(group * POLES_G + piece * PIECE, PIECE), PIECE)

    def pole_copy(h, piece):
        dest = core * 2 + h
        dy = lax.rem(y - dest + NY, NY)
        return pltpu.make_async_remote_copy(
            src_ref=poles.at[:, pl.ds(piece * PIECE, PIECE), pl.ds(h * LANES, LANES)],
            dst_ref=landed.at[:, rows_of(y, piece), :],
            send_sem=pole_send.at[h, piece], recv_sem=pole_recv.at[dy, piece // CORES],
            device_id=(chip * CORES + piece % CORES, dest), device_id_type=MESH)

    def own_ends(h):
        return poles.at[:, :, pl.ds(h * LANES, LANES)], landed.at[:, pl.ds(pl.multiple_of(y * POLES_G, POLES_G), POLES_G), :]

    def own_local(h):
        return pltpu.make_async_copy(*own_ends(h), own_sem)

    def own_remote(h):
        src, dst = own_ends(h)
        return pltpu.make_async_remote_copy(src_ref=src, dst_ref=dst, send_sem=fwd_send.at[0, 0], recv_sem=fwd_recv.at[0, 0],
                                            device_id=sibling, device_id_type=MESH)

    for h in range(2):
        @pl.when(core * 2 + h != y)
        def _():
            for piece in range(PARTS):
                pole_copy(h, piece).start()

        @pl.when(core * 2 + h == y)
        def _():
            own_local(h).start()
            own_remote(h).start()

    small = []
    for n, (src, dst) in enumerate(((weight, wts.at[core]), (basis.at[0:LANES, :], bas.at[core * 2]), (basis.at[LANES:2 * LANES, :], bas.at[core * 2 + 1]))):
        small.append(pltpu.make_async_remote_copy(src_ref=src, dst_ref=dst, send_sem=small_send.at[n], recv_sem=small_recv.at[n],
                                                  device_id=sibling, device_id_type=MESH))
        small[-1].start()
    for copy in small:
        copy.wait()
    for dy in range(NY):
        bas_t[:, dy * LANES:(dy + 1) * LANES] = jnp.transpose(bas[on_ring(dy)].astype(F32)).astype(BF16)

    for copy in idx_copies:
        copy.wait()
    to_smem = pltpu.make_async_copy(all_idx, idx, idx_sem)
    to_smem.start()
    to_smem.wait()

    def spread(group, piece):
        at = group * POLES_G + piece * PIECE
        for k in range(3):
            block = landed[k, pl.ds(pl.multiple_of(at, PIECE), PIECE), :].astype(F32)
            ptab[pl.ds(at * ROW + k, PIECE, stride=ROW), :] = block

    def forward(dy, n):
        where = landed.at[:, rows_of(on_ring(dy), n * CORES + core), :]
        return pltpu.make_async_remote_copy(src_ref=where, dst_ref=where, send_sem=fwd_send.at[dy, n], recv_sem=fwd_recv.at[dy, n],
                                            device_id=sibling, device_id_type=MESH)

    for h in range(2):
        @pl.when(core * 2 + h == y)
        def _():
            own_local(h).wait()
            own_remote(h).wait_send()

    @pl.when(lax.div(y, 2) != core)
    def _():
        own_remote(0).wait_recv()
    for piece in range(PARTS):
        spread(y, piece)

    forwards = []
    for n in range(PARTS // CORES):
        for dy in (1, 3, 2):
            where = landed.at[:, rows_of(on_ring(dy), n * CORES + core), :]
            pltpu.make_async_remote_copy(src_ref=where, dst_ref=where, send_sem=fwd_send.at[dy, n], recv_sem=pole_recv.at[dy, n],
                                         device_id=sibling, device_id_type=MESH).wait_recv()
            forwards.append(forward(dy, n))
            forwards[-1].start()
            spread(on_ring(dy), n * CORES + core)
    for n in range(PARTS // CORES):
        for dy in (1, 3, 2):
            where = landed.at[:, rows_of(on_ring(dy), n * CORES + 1 - core), :]
            pltpu.make_async_remote_copy(src_ref=where, dst_ref=where, send_sem=fwd_send.at[dy, n], recv_sem=fwd_recv.at[dy, n],
                                         device_id=sibling, device_id_type=MESH).wait_recv()
            spread(on_ring(dy), n * CORES + 1 - core)

    def dipoles(b, _):
        row = lax.div(b, 8) * IDX_ROWS + lax.rem(b, 8) * 2
        for u in range(BLOCK):
            plus, minus = idx[row, u], idx[row + 1, u]
            field = ptab[pl.ds(plus, ROW), :] - ptab[pl.ds(minus, ROW), :]
            dtab[pl.ds(pl.multiple_of(b * (BLOCK * ROW), BLOCK * ROW) + u * ROW, ROW), :] = field.astype(BF16).astype(F32)
        return 0

    lax.fori_loop(0, NY * DIP_G // BLOCK, dipoles, 0)

    mine = wts[lax.div(y, 2), pl.ds(lax.rem(y, 2), 1), :]

    def candidates(dy, m):
        block = (on_ring(dy) * CORES + core) * OWN_BLOCKS + m
        row = block_rows[block]
        for u in range(BLOCK):
            near, far = idx[row, u], idx[row + 32, u]
            prod[u * ROW:(u + 1) * ROW, :] = (dtab[pl.ds(near, ROW), :]
                                              * dtab[pl.ds(far, ROW), :])
        total = prod[pl.ds(0, BLOCK, stride=ROW), :] + prod[pl.ds(1, BLOCK, stride=ROW), :] + prod[pl.ds(2, BLOCK, stride=ROW), :]
        sent[dy, pl.ds(pl.multiple_of(m * BLOCK, BLOCK), BLOCK), :] = (total * mine).astype(BF16)

    def sens_copy(dy, s):
        lo, hi = SUBS[s]
        where = pl.ds(lo * BLOCK, (hi - lo) * BLOCK)
        return pltpu.make_async_remote_copy(
            src_ref=sent.at[dy, where, :], dst_ref=came.at[NY - dy, where, :],
            send_sem=sens_send.at[s, dy], recv_sem=sens_recv.at[s, NY - dy],
            device_id=(cells, on_ring(dy)), device_id_type=MESH)

    def part_copy(s, d):
        lo, hi = SUBS[s]
        dx, dz = deltas[d]
        there = back[d]
        where = pl.ds(lo * BLOCK, (hi - lo) * BLOCK)
        to = on_plane(dx, dz)
        return pltpu.make_async_remote_copy(
            src_ref=part.at[to, :, where], dst_ref=got.at[there, :, where],
            send_sem=part_send.at[s, d], recv_sem=part_recv.at[s, there],
            device_id=(to * CORES + core, y), device_id_type=MESH)

    def project(s):
        lo, hi = SUBS[s]
        where = slice(lo * BLOCK, hi * BLOCK)
        for dy in range(1, NY):
            sens_copy(NY - dy, s).wait_recv()
        for m in range(lo, hi):
            rows = slice(m * BLOCK, (m + 1) * BLOCK)
            sens = jnp.concatenate([sent[0, rows, :]] + [came[dy, rows, :] for dy in range(1, NY)], axis=1)
            proj = lax.dot_general(bas_t[...], sens, (((1,), (1,)), ((), ())), preferred_element_type=F32)
            part[:, :, rows] = proj.astype(BF16).reshape(CHIPS, BASIS // CHIPS, BLOCK)
        for d in range(len(deltas)):
            part_copy(s, d).start()

    for s, (lo, hi) in enumerate(SUBS):
        for dy in (1, 2, 3, 0):
            def step(m, _):
                candidates(dy, m)
                return 0
            lax.fori_loop(lo, hi, step, 0)
            if dy:
                sens_copy(dy, s).start()
        if s:
            project(s - 1)
    project(len(SUBS) - 1)

    here = pl.multiple_of((y * CORES + core) * OWN_Q, LANES)
    for s, (lo, hi) in enumerate(SUBS):
        where = slice(lo * BLOCK, hi * BLOCK)
        total = part[chip, :, where].astype(F32)
        for d in range(len(deltas)):
            part_copy(s, back[d]).wait_recv()
            total = total + got[d, :, where].astype(F32)
        out[:, pl.ds(pl.multiple_of(here + lo * BLOCK, LANES), (hi - lo) * BLOCK)] = total.astype(BF16)

    def out_copy(n, dc, dy):
        where = out.at[:, pl.ds(here, OWN_Q)]
        return pltpu.make_async_remote_copy(
            src_ref=where, dst_ref=where, send_sem=out_send.at[n], recv_sem=out_recv.at[dc, (NY - dy) % NY],
            device_id=(chip * CORES + lax.rem(core + dc, CORES), on_ring(dy)), device_id_type=MESH)

    outs = [out_copy(n, dc, dy) for n, (dc, dy) in enumerate((dc, dy) for dc in range(CORES) for dy in range(NY) if dc or dy)]
    for copy in outs:
        copy.start()

    for s in range(len(SUBS)):
        for dy in range(1, NY):
            sens_copy(dy, s).wait_send()
        for d in range(len(deltas)):
            part_copy(s, d).wait_send()
    for copy in forwards:
        copy.wait_send()
    for h in range(2):
        @pl.when(core * 2 + h != y)
        def _():
            for piece in range(PARTS):
                pole_copy(h, piece).wait_send()
    for copy in outs:
        copy.wait()


def on_device(pole_grads, endpoints, current, potential, live_counts, cell_weight, basis):
    poles = jnp.transpose(pole_grads, (1, 0, 2))
    endp = endpoints.T.reshape(2, DIP_G // LANES, LANES).transpose(1, 0, 2).reshape(2 * DIP_G // LANES, LANES)
    weight = jnp.pad(cell_weight.reshape(2, LANES), ((0, 6), (0, 0)))
    starts = jnp.stack([jnp.int32(s) for s in first_blocks(lambda g: live_counts[g])])
    blocks = lax.iota(I32, ALL_Q // BLOCK)
    group = jnp.sum((blocks[:, None] >= starts[None, 1:]).astype(I32), axis=1)
    first = jnp.max(jnp.where(blocks[:, None] >= starts[None, :], starts[None, :], 0), axis=1)
    block_rows = group * IDX_ROWS + 16 + jnp.minimum(blocks - first, Q_G // BLOCK - 1)
    vmem, dma = pltpu.VMEM, pltpu.SemaphoreType.DMA
    packed = pl.pallas_call(
        kernel,
        out_shape=jax.ShapeDtypeStruct((BASIS // CHIPS, ALL_Q + Q_G), BF16),
        in_specs=[pl.BlockSpec(memory_space=pl.ANY)] + [pl.BlockSpec(memory_space=vmem)] * 3
        + [pl.BlockSpec(memory_space=pltpu.SMEM)] + [pl.BlockSpec(memory_space=vmem)] * 2,
        out_specs=pl.BlockSpec(memory_space=vmem),
        scratch_shapes=[
            vmem((3, NY * POLES_G, LANES), BF16),
            vmem((NY * POLES_G * ROW, LANES), F32),
            vmem((NY * DIP_G * ROW, LANES), F32),
            vmem((IDX_ROWS, LANES), I32),
            vmem((NY * IDX_ROWS, LANES), I32),
            pltpu.SMEM((NY * IDX_ROWS, LANES), I32),
            vmem((BLOCK * ROW, LANES), F32),
            vmem((NY, OWN_Q, LANES), BF16),
            vmem((NY, OWN_Q, LANES), BF16),
            vmem((CORES, 8, LANES), F32),
            vmem((NY, LANES, BASIS), BF16),
            vmem((BASIS, NY * LANES), BF16),
            vmem((CHIPS, BASIS // CHIPS, OWN_Q), BF16),
            vmem((CHIPS - 1, BASIS // CHIPS, OWN_Q), BF16),
            dma((2, PARTS)), dma((NY, PARTS // CORES)), dma((NY, PARTS // CORES)), dma((NY, PARTS // CORES)), dma,
            dma((NY,)), dma((NY,)), dma,
            dma((3,)), dma((3,)),
            dma((len(SUBS), NY)), dma((len(SUBS), NY)),
            dma((len(SUBS), CHIPS - 1)), dma((len(SUBS), CHIPS - 1)),
            dma((NY * CORES - 1,)), dma((CORES, NY)),
        ],
        compiler_params=pltpu.CompilerParams(collective_id=0, has_side_effects=True, vmem_limit_bytes=48 * 2**20),
    )(poles, endp, current.reshape(Q_G // LANES, LANES), potential.reshape(Q_G // LANES, LANES), block_rows, weight, basis)

    group = lax.axis_index("holes")
    first = lax.dynamic_index_in_dim(starts, group, keepdims=False) * BLOCK
    limit = lax.dynamic_index_in_dim(live_counts, group, keepdims=False)
    rows = lax.rem(lax.axis_index("cells"), CORES) * 8
    gains = lax.dynamic_slice(packed, (rows, first), (8, Q_G))
    alive = lax.iota(I32, Q_G) < limit
    return jnp.where(alive[None, :], gains, jnp.zeros((), BF16))


def solution(mesh):
    placed = (
        P("holes", None, "cells"),
        P("holes", None),
        P("holes"),
        P("holes"),
        P(),
        P("cells"),
        P("cells", None),
    )
    return jax.shard_map(
        on_device, mesh=mesh, in_specs=placed, out_specs=P("cells", "holes"), check_vma=False
    )
```

```python
import functools

import jax
import jax.numpy as jnp
from jax import lax
from jax.experimental import pallas as pl
from jax.experimental.pallas import tpu as pltpu
from jax.sharding import PartitionSpec as P

F32, BF16, I32 = jnp.float32, jnp.bfloat16, jnp.int32
MESH = pl.DeviceIdType.MESH

LANES = 128
NY, NX, NZ, CORES = 4, 4, 4, 2
CHIPS = NX * NZ
POLES_G, DIP_G, Q_G, BASIS = 1536, 1024, 4096, 256
PARTS = 8
PIECE = POLES_G // PARTS
ROW = 4
BLOCK = 128
LIVE = 10240
OWN_BLOCKS = LIVE // (NY * CORES * BLOCK)
OWN_Q = OWN_BLOCKS * BLOCK
SUBS = ((0, 4), (4, 8), (8, 10))
IDX_ROWS = 80
Q_ROWS = Q_G // LANES
LIST = 16
MARGIN = 24


def kernel(poles, endp, cur, pot, live, weight, basis, out,
           landed, ptab, dtab, all_idx, lists, idx, prod, sent, came, wts, bas, bas_t, part, got, sums, packed, flat,
           in_sem, pole_send, pole_recv, fwd_send, fwd_recv, own_sem, idx_send, idx_recv, idx_sem,
           small_send, small_recv, sens_send, sens_recv, part_send, part_recv, out_send, out_recv):
    cells, y = lax.axis_index("cells"), lax.axis_index("holes")
    core, chip = lax.rem(cells, CORES), lax.div(cells, CORES)
    x, z = lax.div(chip, NZ), lax.rem(chip, NZ)
    sibling = (chip * CORES + 1 - core, y)

    def on_ring(dy):
        return lax.rem(y + dy, NY)

    def on_plane(dx, dz):
        return lax.rem(x + dx, NX) * NZ + lax.rem(z + dz, NZ)

    deltas = [(dx, dz) for dx in range(NX) for dz in range(NZ) if dx or dz]
    back = [deltas.index(((NX - dx) % NX, (NZ - dz) % NZ)) for dx, dz in deltas]

    barrier = pltpu.get_barrier_semaphore()
    for dc in range(CORES):
        for dy in range(NY):
            if dc or dy:
                pl.semaphore_signal(barrier, inc=1, device_id=(chip * CORES + lax.rem(core + dc, CORES), on_ring(dy)), device_id_type=MESH)
    for dx, dz in deltas:
        pl.semaphore_signal(barrier, inc=1, device_id=(on_plane(dx, dz) * CORES + core, y), device_id_type=MESH)

    def idx_ends(n):
        src, rows, size = ((endp, 0, 16), (cur, 16, 32), (pot, 48, 32))[n]
        return src, all_idx.at[pl.ds(pl.multiple_of(MARGIN + y * IDX_ROWS + rows, 8), size), :]

    small_ends = [(weight, wts.at[core]), (basis.at[0:LANES, :], bas.at[core]), (basis.at[LANES:2 * LANES, :], bas.at[CORES + core])]
    ins = [pltpu.make_async_copy(*ends, in_sem.at[n]) for n, ends in enumerate([idx_ends(0), idx_ends(1), idx_ends(2)] + small_ends)]
    for copy in ins:
        copy.start()

    pl.semaphore_wait(barrier, NY * CORES - 1 + len(deltas))

    idx_copies, small = [], []
    for dy in range(1, NY):
        for n in range(3):
            src, dst = idx_ends(n)
            idx_copies.append(pltpu.make_async_remote_copy(
                src_ref=src, dst_ref=dst, send_sem=idx_send.at[dy, n], recv_sem=idx_recv.at[dy, n],
                device_id=(cells, on_ring(dy)), device_id_type=MESH))
    for n, (src, dst) in enumerate(small_ends):
        small.append(pltpu.make_async_remote_copy(src_ref=src, dst_ref=dst, send_sem=small_send.at[n], recv_sem=small_recv.at[n],
                                                  device_id=sibling, device_id_type=MESH))
    for copy in idx_copies + small:
        copy.start()

    def rows_of(group, piece):
        return pl.ds(pl.multiple_of(group * POLES_G + piece * PIECE, PIECE), PIECE)

    def pole_copy(h, piece):
        dest = h * CORES + core
        dy = lax.rem(y - dest + NY, NY)
        return pltpu.make_async_remote_copy(
            src_ref=poles.at[:, pl.ds(piece * PIECE, PIECE), pl.ds(h * LANES, LANES)],
            dst_ref=landed.at[:, rows_of(y, piece), :],
            send_sem=pole_send.at[h, piece], recv_sem=pole_recv.at[dy, piece // CORES],
            device_id=(chip * CORES + piece % CORES, dest), device_id_type=MESH)

    def own_ends(h):
        return poles.at[:, :, pl.ds(h * LANES, LANES)], landed.at[:, pl.ds(pl.multiple_of(y * POLES_G, POLES_G), POLES_G), :]

    def own_local(h):
        return pltpu.make_async_copy(*own_ends(h), own_sem)

    def own_remote(h):
        src, dst = own_ends(h)
        return pltpu.make_async_remote_copy(src_ref=src, dst_ref=dst, send_sem=fwd_send.at[0, 0], recv_sem=fwd_recv.at[0, 0],
                                            device_id=sibling, device_id_type=MESH)

    for h in range(2):
        @pl.when(h * CORES + core != y)
        def _():
            for piece in range(PARTS):
                pole_copy(h, piece).start()

        @pl.when(h * CORES + core == y)
        def _():
            own_local(h).start()
            own_remote(h).start()

    for copy in ins + small:
        copy.wait()
    for dy in range(NY):
        bas_t[:, dy * LANES:(dy + 1) * LANES] = jnp.transpose(bas[on_ring(dy)].astype(F32)).astype(BF16)
    for copy in idx_copies:
        copy.wait()
    starts = [0]
    for g in range(NY - 1):
        starts.append(starts[-1] + live[g])
    for g in range(NY):
        at = MARGIN + g * IDX_ROWS
        lists[g * 16:(g + 1) * 16, :] = all_idx[at:at + 16, :] * ROW
    lane = lax.broadcasted_iota(I32, (LIST, LANES), 1)
    place = lax.broadcasted_iota(I32, (LIST, LANES), 0) * LANES + lane
    for dy in range(NY):
        row = (on_ring(dy) * CORES + core) * OWN_BLOCKS
        for n, offset in enumerate((16, 48)):
            total = jnp.zeros((LIST, LANES), I32)
            for g in range(NY):
                whole, shift = starts[g] // LANES, starts[g] % LANES
                at = MARGIN + g * IDX_ROWS + offset + jnp.clip(row - whole, -LIST, Q_ROWS)
                same = pltpu.roll(all_idx[pl.ds(at, LIST), :], shift, 1)
                before = pltpu.roll(all_idx[pl.ds(at - 1, LIST), :], shift, 1)
                values = jnp.where(lane >= shift, same, before)
                if n == 0:
                    values = values + g * DIP_G
                since = place + (row * LANES - starts[g])
                total = jnp.where((since >= 0) & (since < live[g]), values, total)
            at = NY * 16 + (dy * 2 + n) * LIST
            lists[at:at + LIST, :] = total * ROW
    to_smem = pltpu.make_async_copy(lists, idx, idx_sem)
    to_smem.start()
    to_smem.wait()

    def spread(group, piece):
        at = group * POLES_G + piece * PIECE
        for k in range(3):
            block = landed[k, pl.ds(pl.multiple_of(at, PIECE), PIECE), :].astype(F32)
            ptab[pl.ds(at * ROW + k, PIECE, stride=ROW), :] = block

    def forward(dy, n):
        where = landed.at[:, rows_of(on_ring(dy), n * CORES + core), :]
        return pltpu.make_async_remote_copy(src_ref=where, dst_ref=where, send_sem=fwd_send.at[dy, n], recv_sem=fwd_recv.at[dy, n],
                                            device_id=sibling, device_id_type=MESH)

    for h in range(2):
        @pl.when(h * CORES + core == y)
        def _():
            own_local(h).wait()
            own_remote(h).wait_send()

    @pl.when(lax.rem(y, CORES) != core)
    def _():
        own_remote(0).wait_recv()
    for piece in range(PARTS):
        spread(y, piece)

    forwards = []
    for n in range(PARTS // CORES):
        for dy in (1, 3, 2):
            where = landed.at[:, rows_of(on_ring(dy), n * CORES + core), :]
            pltpu.make_async_remote_copy(src_ref=where, dst_ref=where, send_sem=fwd_send.at[dy, n], recv_sem=pole_recv.at[dy, n],
                                         device_id=sibling, device_id_type=MESH).wait_recv()
            forwards.append(forward(dy, n))
            forwards[-1].start()
            spread(on_ring(dy), n * CORES + core)
    for n in range(PARTS // CORES):
        for dy in (1, 3, 2):
            where = landed.at[:, rows_of(on_ring(dy), n * CORES + 1 - core), :]
            pltpu.make_async_remote_copy(src_ref=where, dst_ref=where, send_sem=fwd_send.at[dy, n], recv_sem=fwd_recv.at[dy, n],
                                         device_id=sibling, device_id_type=MESH).wait_recv()
            spread(on_ring(dy), n * CORES + 1 - core)

    def dipoles(b, _):
        row = b * 2
        for u in range(BLOCK):
            plus, minus = idx[row, u], idx[row + 1, u]
            field = ptab[pl.ds(plus, ROW), :] - ptab[pl.ds(minus, ROW), :]
            dtab[pl.ds(pl.multiple_of(b * (BLOCK * ROW), BLOCK * ROW) + u * ROW, ROW), :] = field.astype(BF16).astype(F32)
        return 0

    lax.fori_loop(0, NY * DIP_G // BLOCK, dipoles, 0)

    mine = wts[lax.rem(y, CORES), pl.ds(lax.div(y, CORES), 1), :]

    def candidates(dy, m):
        row = NY * 16 + dy * 2 * LIST + m
        for u in range(BLOCK):
            near, far = idx[row, u], idx[row + LIST, u]
            prod[u * ROW:(u + 1) * ROW, :] = (dtab[pl.ds(near, ROW), :]
                                              * dtab[pl.ds(far, ROW), :])
        total = prod[pl.ds(0, BLOCK, stride=ROW), :] + prod[pl.ds(1, BLOCK, stride=ROW), :] + prod[pl.ds(2, BLOCK, stride=ROW), :]
        sent[dy, pl.ds(pl.multiple_of(m * BLOCK, BLOCK), BLOCK), :] = (total * mine).astype(BF16)

    def sens_copy(dy, s):
        lo, hi = SUBS[s]
        where = pl.ds(lo * BLOCK, (hi - lo) * BLOCK)
        return pltpu.make_async_remote_copy(
            src_ref=sent.at[dy, where, :], dst_ref=came.at[NY - dy, where, :],
            send_sem=sens_send.at[s, dy], recv_sem=sens_recv.at[s, NY - dy],
            device_id=(cells, on_ring(dy)), device_id_type=MESH)

    def part_copy(s, d):
        lo, hi = SUBS[s]
        dx, dz = deltas[d]
        there = back[d]
        where = pl.ds(lo * BLOCK, (hi - lo) * BLOCK)
        to = on_plane(dx, dz)
        return pltpu.make_async_remote_copy(
            src_ref=part.at[to, :, where], dst_ref=got.at[there, :, where],
            send_sem=part_send.at[s, d], recv_sem=part_recv.at[s, there],
            device_id=(to * CORES + core, y), device_id_type=MESH)

    def project(s):
        lo, hi = SUBS[s]
        where = slice(lo * BLOCK, hi * BLOCK)
        for dy in range(1, NY):
            sens_copy(NY - dy, s).wait_recv()
        for m in range(lo, hi):
            rows = slice(m * BLOCK, (m + 1) * BLOCK)
            sens = jnp.concatenate([sent[0, rows, :]] + [came[dy, rows, :] for dy in range(1, NY)], axis=1)
            proj = lax.dot_general(bas_t[...], sens, (((1,), (1,)), ((), ())), preferred_element_type=F32)
            part[:, :, rows] = proj.astype(BF16).reshape(CHIPS, BASIS // CHIPS, BLOCK)
        for d in range(len(deltas)):
            part_copy(s, d).start()

    peers = [(dc, dy) for dc in range(CORES) for dy in range(NY) if dc or dy]
    here = (y * CORES + core) * (OWN_BLOCKS // 2)

    def out_copy(s, n):
        lo, hi = SUBS[s]
        dc, dy = peers[n]
        to = lax.rem(core + dc, CORES)
        return pltpu.make_async_remote_copy(
            src_ref=sums.at[to, pl.ds(lo // 2, (hi - lo) // 2)], dst_ref=packed.at[pl.ds(here + lo // 2, (hi - lo) // 2)],
            send_sem=out_send.at[s, n], recv_sem=out_recv.at[s, dc, (NY - dy) % NY],
            device_id=(chip * CORES + to, on_ring(dy)), device_id_type=MESH)

    def add_up(s):
        lo, hi = SUBS[s]
        where = slice(lo * BLOCK, hi * BLOCK)
        total = part[chip, :, where].astype(F32)
        for d in range(len(deltas)):
            part_copy(s, back[d]).wait_recv()
            total = total + got[d, :, where].astype(F32)
        for c in range(CORES):
            for m in range(0, hi - lo, 2):
                pair = [total[c * 8:(c + 1) * 8, k * BLOCK:(k + 1) * BLOCK] for k in (m, m + 1)]
                sums[c, (lo + m) // 2] = jnp.concatenate(pair, axis=0).astype(BF16)
        for n in range(len(peers)):
            out_copy(s, n).start()
        for m in range(lo // 2, hi // 2):
            packed[here + m] = sums[core, m]

    for s, (lo, hi) in enumerate(SUBS):
        for dy in (1, 2, 3, 0):
            def step(m, _):
                candidates(dy, m)
                return 0
            lax.fori_loop(lo, hi, step, 0)
            if dy:
                sens_copy(dy, s).start()
        if s:
            project(s - 1)
    add_up(0)
    project(len(SUBS) - 1)
    for s in range(1, len(SUBS)):
        add_up(s)
    for s in range(len(SUBS)):
        for n in range(len(peers)):
            out_copy(s, n).wait_recv()

    for m in range(LIVE // BLOCK // 2):
        pair = packed[m].astype(F32)
        flat[2 * m] = pair[0:8, :]
        flat[2 * m + 1] = pair[8:16, :]
    first = jnp.int32(0)
    for g in range(1, NY):
        first = jnp.where(y == g, starts[g], first)
    whole, shift, limit = first // LANES, first % LANES, live[y]
    lane = lax.broadcasted_iota(I32, (8, LANES), 1)
    kept = LANES - shift
    turn = lax.rem(kept, LANES)
    turned = pltpu.roll(flat[whole], turn, 1)
    for b in range(Q_ROWS):
        then = pltpu.roll(flat[whole + b + 1], turn, 1)
        value = jnp.where(lane < kept, turned, then)
        out[:, b * LANES:(b + 1) * LANES] = jnp.where(lane + b * LANES < limit, value, 0.0)
        turned = then

    for s in range(len(SUBS)):
        for n in range(len(peers)):
            out_copy(s, n).wait_send()
    for s in range(len(SUBS)):
        for dy in range(1, NY):
            sens_copy(dy, s).wait_send()
        for d in range(len(deltas)):
            part_copy(s, d).wait_send()
    for copy in forwards:
        copy.wait_send()
    for h in range(2):
        @pl.when(h * CORES + core != y)
        def _():
            for piece in range(PARTS):
                pole_copy(h, piece).wait_send()


def on_device(pole_grads, endpoints, current, potential, live_counts, cell_weight, basis):
    poles = jnp.transpose(pole_grads, (1, 0, 2))
    endp = endpoints.T.reshape(2, DIP_G // LANES, LANES).transpose(1, 0, 2).reshape(2 * DIP_G // LANES, LANES)
    weight = cell_weight.reshape(2, LANES)
    vmem, dma = pltpu.VMEM, pltpu.SemaphoreType.DMA
    in_hbm = pl.BlockSpec(memory_space=pltpu.HBM)
    gains = pl.pallas_call(
        kernel,
        out_shape=jax.ShapeDtypeStruct((BASIS // CHIPS // CORES, Q_G), F32),
        in_specs=[in_hbm] * 4 + [pl.BlockSpec(memory_space=pltpu.SMEM)] + [in_hbm] * 2,
        out_specs=pl.BlockSpec(memory_space=vmem),
        scratch_shapes=[
            vmem((3, NY * POLES_G, LANES), BF16),
            vmem((NY * POLES_G * ROW, LANES), F32),
            vmem((NY * DIP_G * ROW, LANES), F32),
            vmem((MARGIN + NY * IDX_ROWS + MARGIN, LANES), I32),
            vmem((NY * (16 + 2 * LIST), LANES), I32),
            pltpu.SMEM((NY * (16 + 2 * LIST), LANES), I32),
            vmem((BLOCK * ROW, LANES), F32),
            vmem((NY, OWN_Q, LANES), BF16),
            vmem((NY, OWN_Q, LANES), BF16),
            vmem((CORES, 2, LANES), F32),
            vmem((NY, LANES, BASIS), BF16),
            vmem((BASIS, NY * LANES), BF16),
            vmem((CHIPS, BASIS // CHIPS, OWN_Q), BF16),
            vmem((CHIPS - 1, BASIS // CHIPS, OWN_Q), BF16),
            vmem((CORES, OWN_BLOCKS // 2, 16, BLOCK), BF16),
            vmem((LIVE // BLOCK // 2, 16, BLOCK), BF16),
            vmem((LIVE // BLOCK + Q_ROWS + 1, 8, BLOCK), F32),
            dma((6,)),
            dma((2, PARTS)), dma((NY, PARTS // CORES)), dma((NY, PARTS // CORES)), dma((NY, PARTS // CORES)), dma,
            dma((NY, 3)), dma((NY, 3)), dma,
            dma((3,)), dma((3,)),
            dma((len(SUBS), NY)), dma((len(SUBS), NY)),
            dma((len(SUBS), CHIPS - 1)), dma((len(SUBS), CHIPS - 1)),
            dma((len(SUBS), NY * CORES - 1)), dma((len(SUBS), CORES, NY)),
        ],
        compiler_params=pltpu.CompilerParams(collective_id=0, has_side_effects=True, vmem_limit_bytes=60 * 2**20),
    )(poles, endp, current.reshape(Q_G // LANES, LANES), potential.reshape(Q_G // LANES, LANES), live_counts, weight, basis)
    return gains.astype(BF16)


def solution(mesh):
    placed = (
        P("holes", None, "cells"),
        P("holes", None),
        P("holes"),
        P("holes"),
        P(),
        P("cells"),
        P("cells", None),
    )
    return jax.shard_map(
        on_device, mesh=mesh, in_specs=placed, out_specs=P("cells", "holes"), check_vma=False
    )
```

```python
import functools

import jax
import jax.numpy as jnp
from jax import lax
from jax.experimental import pallas as pl
from jax.experimental.pallas import tpu as pltpu
from jax.sharding import PartitionSpec as P

F32, BF16, I32 = jnp.float32, jnp.bfloat16, jnp.int32
MESH = pl.DeviceIdType.MESH

LANES = 128
NY, NX, NZ, CORES = 4, 4, 4, 2
CHIPS = NX * NZ
POLES_G, DIP_G, Q_G, BASIS = 1536, 1024, 4096, 256
PARTS = 8
PIECE = POLES_G // PARTS
ROW = 4
BLOCK = 128
LIVE = 10240
OWN_BLOCKS = LIVE // (NY * CORES * BLOCK)
OWN_Q = OWN_BLOCKS * BLOCK
SUBS = (("x", 0, 2), ("z", 2, 4), ("x", 4, 6), ("z", 6, 8), ("y", 8, 10))
LAG = 3
PLANE = {"y": ("x", "z"), "x": ("y", "z"), "z": ("x", "y")}
IDX_ROWS = 80
Q_ROWS = Q_G // LANES
LIST = 8
MARGIN = 24


def kernel(poles, endp, cur, pot, live, weight, basis, out,
           landed, ptab, dtab, all_idx, lists, idx, prod, sent, came, wts, bas, bas_far, bas_t, part, got, sums, both, packed, flat,
           in_sem, pole_send, pole_recv, fwd_send, fwd_recv, own_sem, idx_send, idx_recv, idx_sem,
           small_send, small_recv, bas_send, bas_recv, sens_send, sens_recv, part_send, part_recv, pair_send, pair_recv, out_send, out_recv, ring_send, ring_recv):
    cells, y = lax.axis_index("cells"), lax.axis_index("holes")
    core, chip = lax.rem(cells, CORES), lax.div(cells, CORES)
    x, z = lax.div(chip, NZ), lax.rem(chip, NZ)
    sibling = (chip * CORES + 1 - core, y)

    def on_ring(dy):
        return lax.rem(y + dy, NY)

    where_am_i = {"x": x, "y": y, "z": z}

    def at(core_there=core, **steps):
        there = {axis: lax.rem(here + steps.get(axis, 0), 4) for axis, here in where_am_i.items()}
        return (there["x"] * NZ + there["z"]) * CORES + core_there, there["y"]

    deltas = [(i, j) for i in range(4) for j in range(4) if i or j]
    back = [deltas.index(((4 - i) % 4, (4 - j) % 4)) for i, j in deltas]

    barrier = pltpu.get_barrier_semaphore()
    greeted = [at(1 - core, y=dy) for dy in range(NY)]
    greeted += [at(x=i, y=j, z=k) for i in range(NX) for j in range(NY) for k in range(NZ) if (i or j or k) and not (i and j and k)]
    for device in greeted:
        pl.semaphore_signal(barrier, inc=1, device_id=device, device_id_type=MESH)

    def idx_ends(n):
        src, rows, size = ((endp, 0, 16), (cur, 16, 32), (pot, 48, 32))[n]
        return src, all_idx.at[pl.ds(pl.multiple_of(MARGIN + y * IDX_ROWS + rows, 8), size), :]

    small_ends = [(weight, wts.at[core]), (basis.at[0:LANES, :], bas.at[core]), (basis.at[LANES:2 * LANES, :], bas.at[CORES + core])]
    ins = [pltpu.make_async_copy(*ends, in_sem.at[n]) for n, ends in enumerate([idx_ends(0), idx_ends(1), idx_ends(2)] + small_ends)]
    for copy in ins:
        copy.start()

    pl.semaphore_wait(barrier, len(greeted))

    idx_copies, small = [], []
    for dy in range(1, NY):
        for n in range(3):
            src, dst = idx_ends(n)
            idx_copies.append(pltpu.make_async_remote_copy(
                src_ref=src, dst_ref=dst, send_sem=idx_send.at[dy, n], recv_sem=idx_recv.at[dy, n],
                device_id=(cells, on_ring(dy)), device_id_type=MESH))
    for n, (src, dst) in enumerate(small_ends):
        small.append(pltpu.make_async_remote_copy(src_ref=src, dst_ref=dst, send_sem=small_send.at[n], recv_sem=small_recv.at[n],
                                                  device_id=sibling, device_id_type=MESH))
    for copy in idx_copies + small:
        copy.start()

    def rows_of(group, piece):
        return pl.ds(pl.multiple_of(group * POLES_G + piece * PIECE, PIECE), PIECE)

    def pole_copy(h, piece):
        dest = h * CORES + core
        dy = lax.rem(y - dest + NY, NY)
        return pltpu.make_async_remote_copy(
            src_ref=poles.at[:, pl.ds(piece * PIECE, PIECE), pl.ds(h * LANES, LANES)],
            dst_ref=landed.at[:, rows_of(y, piece), :],
            send_sem=pole_send.at[h, piece], recv_sem=pole_recv.at[dy, piece // CORES],
            device_id=(chip * CORES + piece % CORES, dest), device_id_type=MESH)

    def own_ends(h):
        return poles.at[:, :, pl.ds(h * LANES, LANES)], landed.at[:, pl.ds(pl.multiple_of(y * POLES_G, POLES_G), POLES_G), :]

    def own_local(h):
        return pltpu.make_async_copy(*own_ends(h), own_sem)

    def own_remote(h):
        src, dst = own_ends(h)
        return pltpu.make_async_remote_copy(src_ref=src, dst_ref=dst, send_sem=fwd_send.at[0, 0], recv_sem=fwd_recv.at[0, 0],
                                            device_id=sibling, device_id_type=MESH)

    for h in range(2):
        @pl.when(h * CORES + core != y)
        def _():
            for piece in range(PARTS):
                pole_copy(h, piece).start()

        @pl.when(h * CORES + core == y)
        def _():
            own_local(h).start()
            own_remote(h).start()

    for copy in ins + small:
        copy.wait()
    far = []
    for n, axis in enumerate("xz"):
        for d in range(1, 4):
            far.append(pltpu.make_async_remote_copy(src_ref=bas.at[y], dst_ref=bas_far.at[n, 4 - d], send_sem=bas_send.at[n, d], recv_sem=bas_recv.at[n, 4 - d],
                                                    device_id=at(**{axis: d}), device_id_type=MESH))
            far[-1].start()
    for copy in idx_copies + far:
        copy.wait()
    for d in range(4):
        columns = slice(d * LANES, (d + 1) * LANES)
        for n, axis in enumerate("yxz"):
            piece = bas[on_ring(d)] if axis == "y" else bas[y] if d == 0 else bas_far[n - 1, d]
            bas_t[n, :, columns] = jnp.transpose(piece.astype(F32)).astype(BF16)
    starts = [0]
    for g in range(NY - 1):
        starts.append(starts[-1] + live[g])
    for g in range(NY):
        first = MARGIN + g * IDX_ROWS
        lists[g * 16:(g + 1) * 16, :] = all_idx[first:first + 16, :] * ROW
    lane = lax.broadcasted_iota(I32, (LIST, LANES), 1)
    place = lax.broadcasted_iota(I32, (LIST, LANES), 0) * LANES + lane
    for s, (axis, lo, hi) in enumerate(SUBS):
        for d in range(4):
            row = lo * NY * CORES + (lax.rem(where_am_i[axis] + d, 4) * CORES + core) * (hi - lo)
            found = []
            for n, offset in enumerate((16, 48)):
                total = jnp.zeros((LIST, LANES), I32)
                for g in range(NY):
                    whole, shift = starts[g] // LANES, starts[g] % LANES
                    window = MARGIN + g * IDX_ROWS + offset + jnp.clip(row - whole, -LIST, Q_ROWS)
                    same = pltpu.roll(all_idx[pl.ds(window, LIST), :], shift, 1)
                    before = pltpu.roll(all_idx[pl.ds(window - 1, LIST), :], shift, 1)
                    values = jnp.where(lane >= shift, same, before)
                    if n == 0:
                        values = values + g * DIP_G
                    since = place + (row * LANES - starts[g])
                    total = jnp.where((since >= 0) & (since < live[g]), values, total)
                found.append(total[0:4, :])
            first = NY * 16 + (s * 4 + d) * LIST
            lists[first:first + LIST, :] = jnp.concatenate(found, axis=0) * ROW
    to_smem = pltpu.make_async_copy(lists, idx.at[pl.ds(0, lists.shape[0])], idx_sem)
    to_smem.start()
    to_smem.wait()

    def spread(group, piece):
        at = group * POLES_G + piece * PIECE
        for k in range(3):
            block = landed[k, pl.ds(pl.multiple_of(at, PIECE), PIECE), :].astype(F32)
            ptab[pl.ds(at * ROW + k, PIECE, stride=ROW), :] = block

    def forward(dy, n):
        where = landed.at[:, rows_of(on_ring(dy), n * CORES + core), :]
        return pltpu.make_async_remote_copy(src_ref=where, dst_ref=where, send_sem=fwd_send.at[dy, n], recv_sem=fwd_recv.at[dy, n],
                                            device_id=sibling, device_id_type=MESH)

    for h in range(2):
        @pl.when(h * CORES + core == y)
        def _():
            own_local(h).wait()
            own_remote(h).wait_send()

    @pl.when(lax.rem(y, CORES) != core)
    def _():
        own_remote(0).wait_recv()
    for piece in range(PARTS):
        spread(y, piece)

    forwards = []
    for n in range(PARTS // CORES):
        for dy in (1, 3, 2):
            where = landed.at[:, rows_of(on_ring(dy), n * CORES + core), :]
            pltpu.make_async_remote_copy(src_ref=where, dst_ref=where, send_sem=fwd_send.at[dy, n], recv_sem=pole_recv.at[dy, n],
                                         device_id=sibling, device_id_type=MESH).wait_recv()
            forwards.append(forward(dy, n))
            forwards[-1].start()
            spread(on_ring(dy), n * CORES + core)
    for n in range(PARTS // CORES):
        for dy in (1, 3, 2):
            where = landed.at[:, rows_of(on_ring(dy), n * CORES + 1 - core), :]
            pltpu.make_async_remote_copy(src_ref=where, dst_ref=where, send_sem=fwd_send.at[dy, n], recv_sem=fwd_recv.at[dy, n],
                                         device_id=sibling, device_id_type=MESH).wait_recv()
            spread(on_ring(dy), n * CORES + 1 - core)

    def column(u, down):
        return idx.at[pl.ds(down, idx.shape[0] - LIST), pl.ds(u, 1)]

    def dipoles(b, _):
        for k in range(2):
            for u in range(BLOCK):
                plus, minus = column(u, 2 * k)[b * 4, 0], column(u, 2 * k + 1)[b * 4, 0]
                spot = (k * BLOCK + u) * ROW
                prod[spot:spot + ROW, :] = ptab[pl.ds(plus, ROW), :] - ptab[pl.ds(minus, ROW), :]
            done = prod[k * BLOCK * ROW:(k + 1) * BLOCK * ROW, :].astype(BF16).astype(F32)
            dtab[pl.ds(pl.multiple_of((b * 2 + k) * (BLOCK * ROW), BLOCK * ROW), BLOCK * ROW), :] = done
        return 0

    lax.fori_loop(0, NY * DIP_G // BLOCK // 2, dipoles, 0)

    mine = wts[lax.rem(y, CORES), pl.ds(lax.div(y, CORES), 1), :]

    def candidates(s, d):
        row = NY * 16 + (s * 4 + d) * LIST
        for k in range(2):
            for u in range(BLOCK):
                near, far = column(u, k)[row, 0], column(u, k + 4)[row, 0]
                spot = (k * BLOCK + u) * ROW
                prod[spot:spot + ROW, :] = dtab[pl.ds(near, ROW), :] * dtab[pl.ds(far, ROW), :]
            one, two, three = (prod[pl.ds(k * BLOCK * ROW + c, BLOCK, stride=ROW), :] for c in range(3))
            sent[d, pl.ds(pl.multiple_of((s * 2 + k) * BLOCK, BLOCK), BLOCK), :] = ((one + two + three) * mine).astype(BF16)

    def sens_copy(s, d):
        axis, lo, hi = SUBS[s]
        where = pl.ds(lo * BLOCK, (hi - lo) * BLOCK)
        return pltpu.make_async_remote_copy(
            src_ref=sent.at[d, where, :], dst_ref=came.at[4 - d, where, :],
            send_sem=sens_send.at[s, d], recv_sem=sens_recv.at[s, 4 - d],
            device_id=at(**{axis: d}), device_id_type=MESH)

    def share(s, i=0, j=0):
        first, second = (where_am_i[axis] for axis in PLANE[SUBS[s][0]])
        return lax.rem(first + i, 4) * 4 + lax.rem(second + j, 4)

    def part_copy(s, d):
        axis, lo, hi = SUBS[s]
        first, second = PLANE[axis]
        i, j = deltas[d]
        where = pl.ds(lo * BLOCK, (hi - lo) * BLOCK)
        return pltpu.make_async_remote_copy(
            src_ref=part.at[share(s, i, j), :, where], dst_ref=got.at[back[d], :, where],
            send_sem=part_send.at[s, d], recv_sem=part_recv.at[s, back[d]],
            device_id=at(**{first: i, second: j}), device_id_type=MESH)

    def project(s):
        axis, lo, hi = SUBS[s]
        for d in range(1, 4):
            sens_copy(s, 4 - d).wait_recv()
        for m in range(lo, hi):
            rows = slice(m * BLOCK, (m + 1) * BLOCK)
            sens = jnp.concatenate([sent[0, rows, :]] + [came[d, rows, :] for d in range(1, 4)], axis=1)
            proj = lax.dot_general(bas_t["yxz".index(axis)], sens, (((1,), (1,)), ((), ())), preferred_element_type=F32)
            part[:, :, rows] = proj.astype(BF16).reshape(CHIPS, BASIS // CHIPS, BLOCK)
        for d in range(len(deltas)):
            part_copy(s, d).start()

    def pair_copy(s):
        _, lo, hi = SUBS[s]
        half = (hi - lo) // 2
        return pltpu.make_async_remote_copy(
            src_ref=sums.at[0, pl.ds(lo // 2, half)], dst_ref=both.at[pl.ds(lo + core * half, half)],
            send_sem=pair_send.at[s], recv_sem=pair_recv.at[s], device_id=sibling, device_id_type=MESH)

    ring = [(dc, dy) for dc in range(CORES) for dy in range(NY) if dc or dy]

    def ring_copy(s, dc, dy):
        _, lo, hi = SUBS[s]
        half = (hi - lo) // 2
        to = lax.rem(core + dc, CORES)
        return pltpu.make_async_remote_copy(
            src_ref=sums.at[to, pl.ds(lo // 2, half)], dst_ref=packed.at[pl.ds(lo * 4 + (y * CORES + core) * half, half)],
            send_sem=ring_send.at[s, dc, dy], recv_sem=ring_recv.at[s, dc, (NY - dy) % NY],
            device_id=(chip * CORES + to, on_ring(dy)), device_id_type=MESH)

    def add_up(s):
        axis, lo, hi = SUBS[s]
        where = slice(lo * BLOCK, hi * BLOCK)
        total = part[share(s), :, where].astype(F32)
        for d in range(len(deltas)):
            part_copy(s, back[d]).wait_recv()
            total = total + got[d, :, where].astype(F32)
        if axis == "y":
            for m in range(0, hi - lo, 2):
                for c in range(CORES):
                    sums[c, (lo + m) // 2] = jnp.concatenate([total[c * 8:(c + 1) * 8, k * BLOCK:(k + 1) * BLOCK] for k in (m, m + 1)], axis=0).astype(BF16)
            for dc, dy in ring:
                ring_copy(s, dc, dy).start()
            first = lo * 4 + (y * CORES + core) * ((hi - lo) // 2)
            for m in range((hi - lo) // 2):
                packed[first + m] = sums[core, lo // 2 + m]
            return
        for m in range(0, hi - lo, 2):
            pairs = [jnp.concatenate([total[c * 8:(c + 1) * 8, k * BLOCK:(k + 1) * BLOCK] for k in (m, m + 1)], axis=0).astype(BF16) for c in range(CORES)]
            kept = jnp.where(core == 0, pairs[0].astype(F32), pairs[1].astype(F32)).astype(BF16)
            sums[0, (lo + m) // 2] = jnp.where(core == 0, pairs[1].astype(F32), pairs[0].astype(F32)).astype(BF16)
            both[lo + core * ((hi - lo) // 2) + m // 2] = kept
        pair_copy(s).start()

    def out_copy(s, dy, source):
        axis, lo, hi = SUBS[s]
        return pltpu.make_async_remote_copy(
            src_ref=both.at[pl.ds(lo, hi - lo)], dst_ref=packed.at[pl.ds(lo * 4 + where_am_i[axis] * (hi - lo), hi - lo)],
            send_sem=out_send.at[s, dy], recv_sem=out_recv.at[s, source],
            device_id=(share(s) * CORES + core, on_ring(dy)), device_id_type=MESH)

    def send_out(s):
        axis, lo, hi = SUBS[s]
        pair_copy(s).wait_recv()
        for dy in range(1, NY):
            out_copy(s, dy, where_am_i[axis]).start()

        @pl.when(share(s) != chip)
        def _():
            out_copy(s, 0, where_am_i[axis]).start()

        @pl.when(share(s) == chip)
        def _():
            for m in range(hi - lo):
                packed[lo * 4 + where_am_i[axis] * (hi - lo) + m] = both[lo + m]

    def steps(n, _):
        part_now, d = lax.div(n, 4), lax.rem(n + 1, 4)
        candidates(part_now, d)
        for s in range(len(SUBS)):
            @pl.when((part_now == s) & (d != 0))
            def _():
                sens_copy(s, d).start()
        for s in range(len(SUBS) - LAG):
            @pl.when((part_now == s + LAG) & (d == 0))
            def _():
                project(s)
        return 0

    lax.fori_loop(0, 4 * len(SUBS), steps, 0)
    for s in range(len(SUBS) - LAG, len(SUBS)):
        project(s)
    hopping = [s for s, (axis, _, _) in enumerate(SUBS) if axis != "y"]
    for s in range(len(SUBS)):
        add_up(s)
        if s - 1 in hopping:
            send_out(s - 1)
    for s, (axis, lo, hi) in enumerate(SUBS):
        if s not in hopping:
            for dc, dy in ring:
                ring_copy(s, dc, dy).wait_recv()
            continue
        for source in range(4):
            @pl.when((share(s) != chip) | (where_am_i[axis] != source))
            def _():
                out_copy(s, 1, source).wait_recv()

    for m in range(LIVE // BLOCK // 2):
        pair = packed[m].astype(F32)
        flat[2 * m] = pair[0:8, :]
        flat[2 * m + 1] = pair[8:16, :]
    first = jnp.int32(0)
    for g in range(1, NY):
        first = jnp.where(y == g, starts[g], first)
    whole, shift, limit = first // LANES, first % LANES, live[y]
    lane = lax.broadcasted_iota(I32, (8, LANES), 1)
    kept = LANES - shift
    turn = lax.rem(kept, LANES)
    turned = pltpu.roll(flat[whole], turn, 1)
    for b in range(Q_ROWS):
        then = pltpu.roll(flat[whole + b + 1], turn, 1)
        value = jnp.where(lane < kept, turned, then)
        out[:, b * LANES:(b + 1) * LANES] = jnp.where(lane + b * LANES < limit, value, 0.0)
        turned = then

    for s in range(len(SUBS)):
        for d in range(1, 4):
            sens_copy(s, d).wait_send()
        for d in range(len(deltas)):
            part_copy(s, d).wait_send()
        if SUBS[s][0] == "y":
            for dc, dy in ring:
                ring_copy(s, dc, dy).wait_send()
            continue
        pair_copy(s).wait_send()
        for dy in range(1, NY):
            out_copy(s, dy, 0).wait_send()

        @pl.when(share(s) != chip)
        def _():
            out_copy(s, 0, 0).wait_send()
    for copy in forwards:
        copy.wait_send()
    for h in range(2):
        @pl.when(h * CORES + core != y)
        def _():
            for piece in range(PARTS):
                pole_copy(h, piece).wait_send()


def on_device(pole_grads, endpoints, current, potential, live_counts, cell_weight, basis):
    poles = jnp.transpose(pole_grads, (1, 0, 2))
    endp = endpoints.T.reshape(2, DIP_G // LANES, LANES).transpose(1, 0, 2).reshape(2 * DIP_G // LANES, LANES)
    weight = cell_weight.reshape(2, LANES)
    vmem, dma = pltpu.VMEM, pltpu.SemaphoreType.DMA
    in_hbm = pl.BlockSpec(memory_space=pltpu.HBM)
    gains = pl.pallas_call(
        kernel,
        out_shape=jax.ShapeDtypeStruct((BASIS // CHIPS // CORES, Q_G), F32),
        in_specs=[in_hbm] * 4 + [pl.BlockSpec(memory_space=pltpu.SMEM)] + [in_hbm] * 2,
        out_specs=pl.BlockSpec(memory_space=vmem),
        scratch_shapes=[
            vmem((3, NY * POLES_G, LANES), BF16),
            vmem((NY * POLES_G * ROW, LANES), F32),
            vmem((NY * DIP_G * ROW, LANES), F32),
            vmem((MARGIN + NY * IDX_ROWS + MARGIN, LANES), I32),
            vmem((NY * 16 + len(SUBS) * 4 * LIST, LANES), I32),
            pltpu.SMEM((NY * 16 + len(SUBS) * 4 * LIST + LIST, LANES), I32),
            vmem((2 * BLOCK * ROW, LANES), F32),
            vmem((NY, OWN_Q, LANES), BF16),
            vmem((NY, OWN_Q, LANES), BF16),
            vmem((CORES, 2, LANES), F32),
            vmem((NY, LANES, BASIS), BF16),
            vmem((2, 4, LANES, BASIS), BF16),
            vmem((3, BASIS, 4 * LANES), BF16),
            vmem((CHIPS, BASIS // CHIPS, OWN_Q), BF16),
            vmem((CHIPS - 1, BASIS // CHIPS, OWN_Q), BF16),
            vmem((CORES, OWN_BLOCKS // 2, 16, BLOCK), BF16),
            vmem((OWN_BLOCKS, 16, BLOCK), BF16),
            vmem((LIVE // BLOCK // 2, 16, BLOCK), BF16),
            vmem((LIVE // BLOCK + Q_ROWS + 1, 8, BLOCK), F32),
            dma((6,)),
            dma((2, PARTS)), dma((NY, PARTS // CORES)), dma((NY, PARTS // CORES)), dma((NY, PARTS // CORES)), dma,
            dma((NY, 3)), dma((NY, 3)), dma,
            dma((3,)), dma((3,)),
            dma((2, 4)), dma((2, 4)),
            dma((len(SUBS), 4)), dma((len(SUBS), 4)),
            dma((len(SUBS), CHIPS - 1)), dma((len(SUBS), CHIPS - 1)),
            dma((len(SUBS),)), dma((len(SUBS),)),
            dma((len(SUBS), NY)), dma((len(SUBS), NY)),
            dma((len(SUBS), CORES, NY)), dma((len(SUBS), CORES, NY)),
        ],
        compiler_params=pltpu.CompilerParams(collective_id=0, has_side_effects=True, vmem_limit_bytes=60 * 2**20),
    )(poles, endp, current.reshape(Q_G // LANES, LANES), potential.reshape(Q_G // LANES, LANES), live_counts, weight, basis)
    return gains.astype(BF16)


def solution(mesh):
    placed = (
        P("holes", None, "cells"),
        P("holes", None),
        P("holes"),
        P("holes"),
        P(),
        P("cells"),
        P("cells", None),
    )
    return jax.shard_map(
        on_device, mesh=mesh, in_specs=placed, out_specs=P("cells", "holes"), check_vma=False
    )
```

```python
import functools

import jax
import jax.numpy as jnp
from jax import lax
from jax.experimental import pallas as pl
from jax.experimental.pallas import tpu as pltpu
from jax.sharding import PartitionSpec as P

F32, BF16, I32 = jnp.float32, jnp.bfloat16, jnp.int32
MESH = pl.DeviceIdType.MESH

LANES = 128
NY, NX, NZ, CORES = 4, 4, 4, 2
CHIPS = NX * NZ
POLES_G, DIP_G, Q_G, BASIS = 1536, 1024, 4096, 256
PARTS = 8
PIECE = POLES_G // PARTS
ROW = 4
BLOCK = 128
LIVE = 10240
OWN_BLOCKS = LIVE // (NY * CORES * BLOCK)
OWN_Q = OWN_BLOCKS * BLOCK
SUBS = (("y", 0, 2), ("x", 2, 4), ("z", 4, 6), ("x", 6, 8), ("y", 8, 10))
LAG = 3
PLANE = {"y": ("x", "z"), "x": ("y", "z"), "z": ("x", "y")}
IDX_ROWS = 80
Q_ROWS = Q_G // LANES
LIST = LIVE // LANES
MARGIN = 88


def kernel(poles, endp, cur, pot, live, weight, basis, out,
           landed, ptab, dtab, all_idx, lists, idx, prod, sent, came, wts, bas, bas_own, bas_t, part, got, sums, both, packed, flat,
           in_sem, pole_send, pole_recv, fwd_send, fwd_recv, own_sem, idx_send, idx_recv, idx_sem,
           small_send, small_recv, bas_send, bas_recv, sens_send, sens_recv, part_send, part_recv, pair_send, pair_recv, out_send, out_recv, ring_send, ring_recv):
    cells, y = lax.axis_index("cells"), lax.axis_index("holes")
    core, chip = lax.rem(cells, CORES), lax.div(cells, CORES)
    x, z = lax.div(chip, NZ), lax.rem(chip, NZ)
    sibling = (chip * CORES + 1 - core, y)

    def on_ring(dy):
        return lax.rem(y + dy, NY)

    where_am_i = {"x": x, "y": y, "z": z}

    def at(core_there=core, **steps):
        there = {axis: lax.rem(here + steps.get(axis, 0), 4) for axis, here in where_am_i.items()}
        return (there["x"] * NZ + there["z"]) * CORES + core_there, there["y"]

    deltas = [(i, j) for i in range(4) for j in range(4) if i or j]
    back = [deltas.index(((4 - i) % 4, (4 - j) % 4)) for i, j in deltas]

    barrier = pltpu.get_barrier_semaphore()
    greeted = [at(1 - core, y=dy) for dy in range(NY)]
    greeted += [at(x=i, y=j, z=k) for i in range(NX) for j in range(NY) for k in range(NZ) if (i or j or k) and not (i and j and k)]
    for device in greeted:
        pl.semaphore_signal(barrier, inc=1, device_id=device, device_id_type=MESH)

    def idx_ends(n):
        src, rows, size = ((endp, 0, 16), (cur, 16, 32), (pot, 48, 32))[n]
        return src, all_idx.at[pl.ds(pl.multiple_of(MARGIN + y * IDX_ROWS + rows, 8), size), :]

    small_ends = [(weight, wts.at[core]), (basis.at[0:LANES, :], bas.at[core]), (basis.at[LANES:2 * LANES, :], bas.at[CORES + core])]
    ins = [pltpu.make_async_copy(*ends, in_sem.at[n]) for n, ends in enumerate([idx_ends(0), idx_ends(1), idx_ends(2)] + small_ends)]
    for copy in ins:
        copy.start()

    pl.semaphore_wait(barrier, len(greeted))

    idx_copies, small = [], []
    for dy in range(1, NY):
        for n in range(3):
            src, dst = idx_ends(n)
            idx_copies.append(pltpu.make_async_remote_copy(
                src_ref=src, dst_ref=dst, send_sem=idx_send.at[dy, n], recv_sem=idx_recv.at[dy, n],
                device_id=(cells, on_ring(dy)), device_id_type=MESH))
    for n, (src, dst) in enumerate(small_ends):
        small.append(pltpu.make_async_remote_copy(src_ref=src, dst_ref=dst, send_sem=small_send.at[n], recv_sem=small_recv.at[n],
                                                  device_id=sibling, device_id_type=MESH))
    for copy in idx_copies + small:
        copy.start()

    def rows_of(group, piece):
        return pl.ds(pl.multiple_of(group * POLES_G + piece * PIECE, PIECE), PIECE)

    def pole_copy(h, piece):
        dest = h * CORES + core
        dy = lax.rem(y - dest + NY, NY)
        return pltpu.make_async_remote_copy(
            src_ref=poles.at[:, pl.ds(piece * PIECE, PIECE), pl.ds(h * LANES, LANES)],
            dst_ref=landed.at[:, rows_of(y, piece), :],
            send_sem=pole_send.at[h, piece], recv_sem=pole_recv.at[dy, piece // CORES],
            device_id=(chip * CORES + piece % CORES, dest), device_id_type=MESH)

    def own_ends(h):
        return poles.at[:, :, pl.ds(h * LANES, LANES)], landed.at[:, pl.ds(pl.multiple_of(y * POLES_G, POLES_G), POLES_G), :]

    def own_local(h):
        return pltpu.make_async_copy(*own_ends(h), own_sem)

    def own_remote(h):
        src, dst = own_ends(h)
        return pltpu.make_async_remote_copy(src_ref=src, dst_ref=dst, send_sem=fwd_send.at[0, 0], recv_sem=fwd_recv.at[0, 0],
                                            device_id=sibling, device_id_type=MESH)

    for h in range(2):
        @pl.when(h * CORES + core != y)
        def _():
            for piece in range(PARTS):
                pole_copy(h, piece).start()

        @pl.when(h * CORES + core == y)
        def _():
            own_local(h).start()
            own_remote(h).start()

    for copy in ins + small:
        copy.wait()
    bas_own[...] = jnp.transpose(bas[y].astype(F32)).astype(BF16)
    far = []
    for n, axis in enumerate("yxz"):
        bas_t[n, :, 0:LANES] = bas_own[...]
        for d in range(1, 4):
            if axis == "y":
                bas_t[n, :, d * LANES:(d + 1) * LANES] = jnp.transpose(bas[on_ring(d)].astype(F32)).astype(BF16)
                continue
            far.append(pltpu.make_async_remote_copy(
                src_ref=bas_own, dst_ref=bas_t.at[n, :, pl.ds((4 - d) * LANES, LANES)], send_sem=bas_send.at[n, d], recv_sem=bas_recv.at[n, 4 - d],
                device_id=at(**{axis: d}), device_id_type=MESH))
            far[-1].start()
    for copy in idx_copies:
        copy.wait()
    starts = [0]
    for g in range(NY - 1):
        starts.append(starts[-1] + live[g])
    for g in range(NY):
        first = MARGIN + g * IDX_ROWS
        lists[g * 16:(g + 1) * 16, :] = all_idx[first:first + 16, :] * ROW
    lane = lax.broadcasted_iota(I32, (LIST, LANES), 1)
    place = lax.broadcasted_iota(I32, (LIST, LANES), 0) * LANES + lane
    for n, offset in enumerate((16, 48)):
        total = jnp.zeros((LIST, LANES), I32)
        for g in range(NY):
            whole, shift = starts[g] // LANES, starts[g] % LANES
            window = MARGIN + g * IDX_ROWS + offset - whole
            same = pltpu.roll(all_idx[pl.ds(window, LIST), :], shift, 1)
            before = pltpu.roll(all_idx[pl.ds(window - 1, LIST), :], shift, 1)
            values = jnp.where(lane >= shift, same, before)
            if n == 0:
                values = values + g * DIP_G
            since = place - starts[g]
            total = jnp.where((since >= 0) & (since < live[g]), values, total)
        lists[NY * 16 + n * LIST:NY * 16 + (n + 1) * LIST, :] = total * ROW
    to_smem = pltpu.make_async_copy(lists, idx.at[pl.ds(0, lists.shape[0]), :], idx_sem)
    to_smem.start()
    to_smem.wait()

    def spread(group, piece):
        at = group * POLES_G + piece * PIECE
        for k in range(3):
            block = landed[k, pl.ds(pl.multiple_of(at, PIECE), PIECE), :].astype(F32)
            ptab[pl.ds(at * ROW + k, PIECE, stride=ROW), :] = block

    def forward(dy, n):
        where = landed.at[:, rows_of(on_ring(dy), n * CORES + core), :]
        return pltpu.make_async_remote_copy(src_ref=where, dst_ref=where, send_sem=fwd_send.at[dy, n], recv_sem=fwd_recv.at[dy, n],
                                            device_id=sibling, device_id_type=MESH)

    for h in range(2):
        @pl.when(h * CORES + core == y)
        def _():
            own_local(h).wait()
            own_remote(h).wait_send()

    @pl.when(lax.rem(y, CORES) != core)
    def _():
        own_remote(0).wait_recv()
    for piece in range(PARTS):
        spread(y, piece)

    forwards = []

    def from_sibling(dy, n):
        forward_there = landed.at[:, rows_of(on_ring(dy), n * CORES + 1 - core), :]
        pltpu.make_async_remote_copy(src_ref=forward_there, dst_ref=forward_there, send_sem=fwd_send.at[dy, n], recv_sem=fwd_recv.at[dy, n],
                                     device_id=sibling, device_id_type=MESH).wait_recv()
        spread(on_ring(dy), n * CORES + 1 - core)

    for n in range(PARTS // CORES):
        for dy in (1, 3, 2):
            where = landed.at[:, rows_of(on_ring(dy), n * CORES + core), :]
            pltpu.make_async_remote_copy(src_ref=where, dst_ref=where, send_sem=fwd_send.at[dy, n], recv_sem=pole_recv.at[dy, n],
                                         device_id=sibling, device_id_type=MESH).wait_recv()
            forwards.append(forward(dy, n))
            forwards[-1].start()
            spread(on_ring(dy), n * CORES + core)
            if n:
                from_sibling(dy, n - 1)
    for dy in (1, 3, 2):
        from_sibling(dy, PARTS // CORES - 1)

    def column(u, down):
        return idx.at[pl.ds(down, idx.shape[0] - LIST - 2), pl.ds(u, 1)]

    def dipoles(b, _):
        for k in range(2):
            for u in range(BLOCK):
                plus, minus = column(u, 2 * k)[b * 4, 0], column(u, 2 * k + 1)[b * 4, 0]
                spot = (k * BLOCK + u) * ROW
                prod[spot:spot + ROW, :] = ptab[pl.ds(plus, ROW), :] - ptab[pl.ds(minus, ROW), :]
            done = prod[k * BLOCK * ROW:(k + 1) * BLOCK * ROW, :].astype(BF16).astype(F32)
            dtab[pl.ds(pl.multiple_of((b * 2 + k) * (BLOCK * ROW), BLOCK * ROW), BLOCK * ROW), :] = done
        return 0

    lax.fori_loop(0, NY * DIP_G // BLOCK // 2, dipoles, 0)

    mine = wts[lax.rem(y, CORES), pl.ds(lax.div(y, CORES), 1), :]

    def candidates(s, d):
        there = jnp.int32(0)
        for n, (axis, _, _) in enumerate(SUBS):
            there = jnp.where(s == n, where_am_i[axis], there)
        row = NY * 16 + s * 16 + (lax.rem(there + d, 4) * CORES + core) * 2
        for k in range(2):
            for u in range(BLOCK):
                near, far = column(u, k)[row, 0], column(u, k + LIST)[row, 0]
                spot = (k * BLOCK + u) * ROW
                prod[spot:spot + ROW, :] = dtab[pl.ds(near, ROW), :] * dtab[pl.ds(far, ROW), :]
            one, two, three = (prod[pl.ds(k * BLOCK * ROW + c, BLOCK, stride=ROW), :] for c in range(3))
            sent[d, pl.ds(pl.multiple_of((s * 2 + k) * BLOCK, BLOCK), BLOCK), :] = ((one + two + three) * mine).astype(BF16)

    def sens_copy(s, d):
        axis, lo, hi = SUBS[s]
        where = pl.ds(lo * BLOCK, (hi - lo) * BLOCK)
        return pltpu.make_async_remote_copy(
            src_ref=sent.at[d, where, :], dst_ref=came.at[4 - d, where, :],
            send_sem=sens_send.at[s, d], recv_sem=sens_recv.at[s, 4 - d],
            device_id=at(**{axis: d}), device_id_type=MESH)

    def share(s, i=0, j=0):
        first, second = (where_am_i[axis] for axis in PLANE[SUBS[s][0]])
        return lax.rem(first + i, 4) * 4 + lax.rem(second + j, 4)

    def part_copy(s, d):
        axis, lo, hi = SUBS[s]
        first, second = PLANE[axis]
        i, j = deltas[d]
        where = pl.ds(lo * BLOCK, (hi - lo) * BLOCK)
        return pltpu.make_async_remote_copy(
            src_ref=part.at[share(s, i, j), :, where], dst_ref=got.at[back[d], :, where],
            send_sem=part_send.at[s, d], recv_sem=part_recv.at[s, back[d]],
            device_id=at(**{first: i, second: j}), device_id_type=MESH)

    def project(s):
        axis, lo, hi = SUBS[s]
        for d in range(1, 4):
            sens_copy(s, 4 - d).wait_recv()
        for m in range(lo, hi):
            rows = slice(m * BLOCK, (m + 1) * BLOCK)
            sens = jnp.concatenate([sent[0, rows, :]] + [came[d, rows, :] for d in range(1, 4)], axis=1)
            proj = lax.dot_general(bas_t["yxz".index(axis)], sens, (((1,), (1,)), ((), ())), preferred_element_type=F32)
            part[:, :, rows] = proj.astype(BF16).reshape(CHIPS, BASIS // CHIPS, BLOCK)
        for d in range(len(deltas)):
            part_copy(s, d).start()

    def pair_copy(s):
        _, lo, hi = SUBS[s]
        half = (hi - lo) // 2
        return pltpu.make_async_remote_copy(
            src_ref=sums.at[0, pl.ds(lo // 2, half)], dst_ref=both.at[pl.ds(lo + core * half, half)],
            send_sem=pair_send.at[s], recv_sem=pair_recv.at[s], device_id=sibling, device_id_type=MESH)

    ring = [(dc, dy) for dc in range(CORES) for dy in range(NY) if dc or dy]

    def ring_copy(s, dc, dy):
        _, lo, hi = SUBS[s]
        half = (hi - lo) // 2
        to = lax.rem(core + dc, CORES)
        return pltpu.make_async_remote_copy(
            src_ref=sums.at[to, pl.ds(lo // 2, half)], dst_ref=packed.at[pl.ds(lo * 4 + (y * CORES + core) * half, half)],
            send_sem=ring_send.at[s, dc, dy], recv_sem=ring_recv.at[s, dc, (NY - dy) % NY],
            device_id=(chip * CORES + to, on_ring(dy)), device_id_type=MESH)

    def add_up(s):
        axis, lo, hi = SUBS[s]
        where = slice(lo * BLOCK, hi * BLOCK)
        total = part[share(s), :, where].astype(F32)
        for d in range(len(deltas)):
            part_copy(s, back[d]).wait_recv()
            total = total + got[d, :, where].astype(F32)
        if axis == "y":
            for m in range(0, hi - lo, 2):
                for c in range(CORES):
                    sums[c, (lo + m) // 2] = jnp.concatenate([total[c * 8:(c + 1) * 8, k * BLOCK:(k + 1) * BLOCK] for k in (m, m + 1)], axis=0).astype(BF16)
            for dc, dy in ring:
                ring_copy(s, dc, dy).start()
            first = lo * 4 + (y * CORES + core) * ((hi - lo) // 2)
            for m in range((hi - lo) // 2):
                packed[first + m] = sums[core, lo // 2 + m]
            return
        for m in range(0, hi - lo, 2):
            pairs = [jnp.concatenate([total[c * 8:(c + 1) * 8, k * BLOCK:(k + 1) * BLOCK] for k in (m, m + 1)], axis=0).astype(BF16) for c in range(CORES)]
            kept = jnp.where(core == 0, pairs[0].astype(F32), pairs[1].astype(F32)).astype(BF16)
            sums[0, (lo + m) // 2] = jnp.where(core == 0, pairs[1].astype(F32), pairs[0].astype(F32)).astype(BF16)
            both[lo + core * ((hi - lo) // 2) + m // 2] = kept
        pair_copy(s).start()

    def out_copy(s, dy, source):
        axis, lo, hi = SUBS[s]
        return pltpu.make_async_remote_copy(
            src_ref=both.at[pl.ds(lo, hi - lo)], dst_ref=packed.at[pl.ds(lo * 4 + where_am_i[axis] * (hi - lo), hi - lo)],
            send_sem=out_send.at[s, dy], recv_sem=out_recv.at[s, source],
            device_id=(share(s) * CORES + core, on_ring(dy)), device_id_type=MESH)

    def send_out(s):
        axis, lo, hi = SUBS[s]
        pair_copy(s).wait_recv()
        for dy in range(1, NY):
            out_copy(s, dy, where_am_i[axis]).start()

        @pl.when(share(s) != chip)
        def _():
            out_copy(s, 0, where_am_i[axis]).start()

        @pl.when(share(s) == chip)
        def _():
            for m in range(hi - lo):
                packed[lo * 4 + where_am_i[axis] * (hi - lo) + m] = both[lo + m]

    def steps(n, _):
        part_now, d = lax.div(n, 4), lax.rem(n + 1, 4)
        candidates(part_now, d)
        for s in range(len(SUBS)):
            @pl.when((part_now == s) & (d != 0))
            def _():
                sens_copy(s, d).start()
        for s in range(len(SUBS) - LAG):
            @pl.when((part_now == s + LAG) & (d == 0))
            def _():
                project(s)
        return 0

    for copy in far:
        copy.wait()
    lax.fori_loop(0, 4 * len(SUBS), steps, 0)
    for s in range(len(SUBS) - LAG, len(SUBS)):
        project(s)
    hopping = [s for s, (axis, _, _) in enumerate(SUBS) if axis != "y"]
    for s in range(len(SUBS)):
        add_up(s)
        if s - 1 in hopping:
            send_out(s - 1)
    for s in range(len(SUBS)):
        for d in range(1, 4):
            sens_copy(s, d).wait_send()
        for d in range(len(deltas)):
            part_copy(s, d).wait_send()
    for copy in forwards:
        copy.wait_send()
    for h in range(2):
        @pl.when(h * CORES + core != y)
        def _():
            for piece in range(PARTS):
                pole_copy(h, piece).wait_send()
    for s, (axis, lo, hi) in enumerate(SUBS):
        if s not in hopping:
            for dc, dy in ring:
                ring_copy(s, dc, dy).wait_recv()
            continue
        for source in range(4):
            @pl.when((share(s) != chip) | (where_am_i[axis] != source))
            def _():
                out_copy(s, 1, source).wait_recv()

    for m in range(LIVE // BLOCK // 2):
        pair = packed[m].astype(F32)
        flat[2 * m] = pair[0:8, :]
        flat[2 * m + 1] = pair[8:16, :]
    first = jnp.int32(0)
    for g in range(1, NY):
        first = jnp.where(y == g, starts[g], first)
    whole, shift, limit = first // LANES, first % LANES, live[y]
    lane = lax.broadcasted_iota(I32, (8, LANES), 1)
    kept = LANES - shift
    turn = lax.rem(kept, LANES)
    turned = pltpu.roll(flat[whole], turn, 1)
    for b in range(Q_ROWS):
        then = pltpu.roll(flat[whole + b + 1], turn, 1)
        value = jnp.where(lane < kept, turned, then)
        out[:, b * LANES:(b + 1) * LANES] = jnp.where(lane + b * LANES < limit, value, 0.0)
        turned = then

    for s in range(len(SUBS)):
        if s not in hopping:
            for dc, dy in ring:
                ring_copy(s, dc, dy).wait_send()
            continue
        pair_copy(s).wait_send()
        for dy in range(1, NY):
            out_copy(s, dy, 0).wait_send()

        @pl.when(share(s) != chip)
        def _():
            out_copy(s, 0, 0).wait_send()


def on_device(pole_grads, endpoints, current, potential, live_counts, cell_weight, basis):
    poles = jnp.transpose(pole_grads, (1, 0, 2))
    endp = endpoints.T.reshape(2, DIP_G // LANES, LANES).transpose(1, 0, 2).reshape(2 * DIP_G // LANES, LANES)
    weight = cell_weight.reshape(2, LANES)
    vmem, dma = pltpu.VMEM, pltpu.SemaphoreType.DMA
    in_hbm = pl.BlockSpec(memory_space=pltpu.HBM)
    gains = pl.pallas_call(
        kernel,
        out_shape=jax.ShapeDtypeStruct((BASIS // CHIPS // CORES, Q_G), F32),
        in_specs=[in_hbm] * 4 + [pl.BlockSpec(memory_space=pltpu.SMEM)] + [in_hbm] * 2,
        out_specs=pl.BlockSpec(memory_space=vmem),
        scratch_shapes=[
            vmem((3, NY * POLES_G, LANES), BF16),
            vmem((NY * POLES_G * ROW, LANES), F32),
            vmem((NY * DIP_G * ROW, LANES), F32),
            vmem((MARGIN + NY * IDX_ROWS + MARGIN, LANES), I32),
            vmem((NY * 16 + 2 * LIST, LANES), I32),
            pltpu.SMEM((NY * 16 + 2 * LIST + 2, LANES), I32),
            vmem((2 * BLOCK * ROW, LANES), F32),
            vmem((NY, OWN_Q, LANES), BF16),
            vmem((NY, OWN_Q, LANES), BF16),
            vmem((CORES, 2, LANES), F32),
            vmem((NY, LANES, BASIS), BF16),
            vmem((BASIS, LANES), BF16),
            vmem((3, BASIS, 4 * LANES), BF16),
            vmem((CHIPS, BASIS // CHIPS, OWN_Q), BF16),
            vmem((CHIPS - 1, BASIS // CHIPS, OWN_Q), BF16),
            vmem((CORES, OWN_BLOCKS // 2, 16, BLOCK), BF16),
            vmem((OWN_BLOCKS, 16, BLOCK), BF16),
            vmem((LIVE // BLOCK // 2, 16, BLOCK), BF16),
            vmem((LIVE // BLOCK + Q_ROWS + 1, 8, BLOCK), F32),
            dma((6,)),
            dma((2, PARTS)), dma((NY, PARTS // CORES)), dma((NY, PARTS // CORES)), dma((NY, PARTS // CORES)), dma,
            dma((NY, 3)), dma((NY, 3)), dma,
            dma((3,)), dma((3,)),
            dma((3, 4)), dma((3, 4)),
            dma((len(SUBS), 4)), dma((len(SUBS), 4)),
            dma((len(SUBS), CHIPS - 1)), dma((len(SUBS), CHIPS - 1)),
            dma((len(SUBS),)), dma((len(SUBS),)),
            dma((len(SUBS), NY)), dma((len(SUBS), NY)),
            dma((len(SUBS), CORES, NY)), dma((len(SUBS), CORES, NY)),
        ],
        compiler_params=pltpu.CompilerParams(collective_id=0, has_side_effects=True, vmem_limit_bytes=60 * 2**20),
    )(poles, endp, current.reshape(Q_G // LANES, LANES), potential.reshape(Q_G // LANES, LANES), live_counts, weight, basis)
    return gains.astype(BF16)


def solution(mesh):
    placed = (
        P("holes", None, "cells"),
        P("holes", None),
        P("holes"),
        P("holes"),
        P(),
        P("cells"),
        P("cells", None),
    )
    return jax.shard_map(
        on_device, mesh=mesh, in_specs=placed, out_specs=P("cells", "holes"), check_vma=False
    )
```

```python
import functools

import jax
import jax.numpy as jnp
from jax import lax
from jax.experimental import pallas as pl
from jax.experimental.pallas import tpu as pltpu
from jax.sharding import PartitionSpec as P

F32, BF16, I32 = jnp.float32, jnp.bfloat16, jnp.int32
MESH = pl.DeviceIdType.MESH

LANES = 128
NY, NX, NZ, CORES = 4, 4, 4, 2
CHIPS = NX * NZ
POLES_G, DIP_G, Q_G, BASIS = 1536, 1024, 4096, 256
PARTS = 8
PIECE = POLES_G // PARTS
ROW = 4
BLOCK = 128
LIVE = 10240
OWN_BLOCKS = LIVE // (NY * CORES * BLOCK)
OWN_Q = OWN_BLOCKS * BLOCK
SUBS = (("y", 0, 2), ("x", 2, 4), ("z", 4, 6), ("x", 6, 8), ("y", 8, 10))
LAG = 4
PLANE = {"y": ("x", "z"), "x": ("y", "z"), "z": ("x", "y")}
IDX_ROWS = 80
Q_ROWS = Q_G // LANES
LIST = LIVE // LANES
MARGIN = 88


def kernel(poles, endp, cur, pot, live, weight, basis, out,
           landed, ptab, dtab, all_idx, lists, idx, prod, sent, came, wts, bas, bas_own, bas_t, part, got, sums, both, packed, flat,
           in_sem, pole_send, pole_recv, fwd_send, fwd_recv, own_sem, idx_send, idx_recv, idx_sem,
           small_send, small_recv, bas_send, bas_recv, sens_send, sens_recv, part_send, part_recv, pair_send, pair_recv, out_send, out_recv, ring_send, ring_recv):
    cells, y = lax.axis_index("cells"), lax.axis_index("holes")
    core, chip = lax.rem(cells, CORES), lax.div(cells, CORES)
    x, z = lax.div(chip, NZ), lax.rem(chip, NZ)
    sibling = (chip * CORES + 1 - core, y)

    def on_ring(dy):
        return lax.rem(y + dy, NY)

    where_am_i = {"x": x, "y": y, "z": z}

    def at(core_there=core, **steps):
        there = {axis: lax.rem(here + steps.get(axis, 0), 4) for axis, here in where_am_i.items()}
        return (there["x"] * NZ + there["z"]) * CORES + core_there, there["y"]

    deltas = [(i, j) for i in range(4) for j in range(4) if i or j]
    back = [deltas.index(((4 - i) % 4, (4 - j) % 4)) for i, j in deltas]

    barrier = pltpu.get_barrier_semaphore()
    greeted = [at(1 - core, y=dy) for dy in range(NY)]
    greeted += [at(x=i, y=j, z=k) for i in range(NX) for j in range(NY) for k in range(NZ) if (i or j or k) and not (i and j and k)]
    for device in greeted:
        pl.semaphore_signal(barrier, inc=1, device_id=device, device_id_type=MESH)

    def idx_ends(n):
        src, rows, size = ((endp, 0, 16), (cur, 16, 32), (pot, 48, 32))[n]
        return src, all_idx.at[pl.ds(pl.multiple_of(MARGIN + y * IDX_ROWS + rows, 8), size), :]

    small_ends = [(weight, wts.at[core]), (basis.at[0:LANES, :], bas.at[core]), (basis.at[LANES:2 * LANES, :], bas.at[CORES + core])]
    ins = [pltpu.make_async_copy(*ends, in_sem.at[n]) for n, ends in enumerate([idx_ends(0), idx_ends(1), idx_ends(2)] + small_ends)]
    for copy in ins:
        copy.start()

    pl.semaphore_wait(barrier, len(greeted))

    idx_copies, small = [], []
    for dy in range(1, NY):
        for n in range(3):
            src, dst = idx_ends(n)
            idx_copies.append(pltpu.make_async_remote_copy(
                src_ref=src, dst_ref=dst, send_sem=idx_send.at[dy, n], recv_sem=idx_recv.at[dy, n],
                device_id=(cells, on_ring(dy)), device_id_type=MESH))
    for n, (src, dst) in enumerate(small_ends):
        small.append(pltpu.make_async_remote_copy(src_ref=src, dst_ref=dst, send_sem=small_send.at[n], recv_sem=small_recv.at[n],
                                                  device_id=sibling, device_id_type=MESH))
    for copy in idx_copies + small:
        copy.start()

    def rows_of(group, piece):
        return pl.ds(pl.multiple_of(group * POLES_G + piece * PIECE, PIECE), PIECE)

    def pole_copy(h, piece):
        dest = h * CORES + core
        dy = lax.rem(y - dest + NY, NY)
        return pltpu.make_async_remote_copy(
            src_ref=poles.at[:, pl.ds(piece * PIECE, PIECE), pl.ds(h * LANES, LANES)],
            dst_ref=landed.at[:, rows_of(y, piece), :],
            send_sem=pole_send.at[h, piece], recv_sem=pole_recv.at[dy, piece // CORES],
            device_id=(chip * CORES + piece % CORES, dest), device_id_type=MESH)

    def own_ends(h):
        return poles.at[:, :, pl.ds(h * LANES, LANES)], landed.at[:, pl.ds(pl.multiple_of(y * POLES_G, POLES_G), POLES_G), :]

    def own_local(h):
        return pltpu.make_async_copy(*own_ends(h), own_sem)

    def own_remote(h):
        src, dst = own_ends(h)
        return pltpu.make_async_remote_copy(src_ref=src, dst_ref=dst, send_sem=fwd_send.at[0, 0], recv_sem=fwd_recv.at[0, 0],
                                            device_id=sibling, device_id_type=MESH)

    for h in range(2):
        @pl.when(h * CORES + core != y)
        def _():
            for piece in range(PARTS):
                pole_copy(h, piece).start()

        @pl.when(h * CORES + core == y)
        def _():
            own_local(h).start()
            own_remote(h).start()

    for copy in ins + small:
        copy.wait()
    bas_own[...] = jnp.transpose(bas[y].astype(F32)).astype(BF16)
    far = []
    for n, axis in enumerate("yxz"):
        bas_t[n, :, 0:LANES] = bas_own[...]
        for d in range(1, 4):
            if axis == "y":
                bas_t[n, :, d * LANES:(d + 1) * LANES] = jnp.transpose(bas[on_ring(d)].astype(F32)).astype(BF16)
                continue
            far.append(pltpu.make_async_remote_copy(
                src_ref=bas_own, dst_ref=bas_t.at[n, :, pl.ds((4 - d) * LANES, LANES)], send_sem=bas_send.at[n, d], recv_sem=bas_recv.at[n, 4 - d],
                device_id=at(**{axis: d}), device_id_type=MESH))
            far[-1].start()
    for copy in idx_copies:
        copy.wait()
    starts = [0]
    for g in range(NY - 1):
        starts.append(starts[-1] + live[g])
    for g in range(NY):
        first = MARGIN + g * IDX_ROWS
        lists[g * 16:(g + 1) * 16, :] = all_idx[first:first + 16, :] * ROW
    lane = lax.broadcasted_iota(I32, (LIST, LANES), 1)
    place = lax.broadcasted_iota(I32, (LIST, LANES), 0) * LANES + lane
    for n, offset in enumerate((16, 48)):
        total = jnp.zeros((LIST, LANES), I32)
        for g in range(NY):
            whole, shift = starts[g] // LANES, starts[g] % LANES
            window = MARGIN + g * IDX_ROWS + offset - whole
            same = pltpu.roll(all_idx[pl.ds(window, LIST), :], shift, 1)
            before = pltpu.roll(all_idx[pl.ds(window - 1, LIST), :], shift, 1)
            values = jnp.where(lane >= shift, same, before)
            if n == 0:
                values = values + g * DIP_G
            since = place - starts[g]
            total = jnp.where((since >= 0) & (since < live[g]), values, total)
        lists[NY * 16 + n * LIST:NY * 16 + (n + 1) * LIST, :] = total * ROW
    to_smem = pltpu.make_async_copy(lists, idx.at[pl.ds(0, lists.shape[0]), :], idx_sem)
    to_smem.start()
    to_smem.wait()

    def spread(group, piece):
        at = group * POLES_G + piece * PIECE
        for k in range(3):
            block = landed[k, pl.ds(pl.multiple_of(at, PIECE), PIECE), :].astype(F32)
            ptab[pl.ds(at * ROW + k, PIECE, stride=ROW), :] = block

    def forward(dy, n):
        where = landed.at[:, rows_of(on_ring(dy), n * CORES + core), :]
        return pltpu.make_async_remote_copy(src_ref=where, dst_ref=where, send_sem=fwd_send.at[dy, n], recv_sem=fwd_recv.at[dy, n],
                                            device_id=sibling, device_id_type=MESH)

    for h in range(2):
        @pl.when(h * CORES + core == y)
        def _():
            own_local(h).wait()
            own_remote(h).wait_send()

    @pl.when(lax.rem(y, CORES) != core)
    def _():
        own_remote(0).wait_recv()
    for piece in range(PARTS):
        spread(y, piece)

    forwards = []

    def from_sibling(dy, n):
        forward_there = landed.at[:, rows_of(on_ring(dy), n * CORES + 1 - core), :]
        pltpu.make_async_remote_copy(src_ref=forward_there, dst_ref=forward_there, send_sem=fwd_send.at[dy, n], recv_sem=fwd_recv.at[dy, n],
                                     device_id=sibling, device_id_type=MESH).wait_recv()
        spread(on_ring(dy), n * CORES + 1 - core)

    for n in range(PARTS // CORES):
        for dy in (1, 3, 2):
            where = landed.at[:, rows_of(on_ring(dy), n * CORES + core), :]
            pltpu.make_async_remote_copy(src_ref=where, dst_ref=where, send_sem=fwd_send.at[dy, n], recv_sem=pole_recv.at[dy, n],
                                         device_id=sibling, device_id_type=MESH).wait_recv()
            forwards.append(forward(dy, n))
            forwards[-1].start()
            spread(on_ring(dy), n * CORES + core)
            if n:
                from_sibling(dy, n - 1)
    for dy in (1, 3, 2):
        from_sibling(dy, PARTS // CORES - 1)

    def column(u, down):
        return idx.at[pl.ds(down, idx.shape[0] - LIST - 2), pl.ds(u, 1)]

    def dipoles(b, _):
        for k in range(2):
            for u in range(BLOCK):
                plus, minus = column(u, 2 * k)[b * 4, 0], column(u, 2 * k + 1)[b * 4, 0]
                spot = (k * BLOCK + u) * ROW
                prod[spot:spot + ROW, :] = ptab[pl.ds(plus, ROW), :] - ptab[pl.ds(minus, ROW), :]
            done = prod[k * BLOCK * ROW:(k + 1) * BLOCK * ROW, :].astype(BF16).astype(F32)
            dtab[pl.ds(pl.multiple_of((b * 2 + k) * (BLOCK * ROW), BLOCK * ROW), BLOCK * ROW), :] = done
        return 0

    lax.fori_loop(0, NY * DIP_G // BLOCK // 2, dipoles, 0)

    mine = wts[lax.rem(y, CORES), pl.ds(lax.div(y, CORES), 1), :]

    def candidates(s, d):
        there = jnp.int32(0)
        for n, (axis, _, _) in enumerate(SUBS):
            there = jnp.where(s == n, where_am_i[axis], there)
        row = NY * 16 + s * 16 + (lax.rem(there + d, 4) * CORES + core) * 2
        for k in range(2):
            for u in range(BLOCK):
                near, far = column(u, k)[row, 0], column(u, k + LIST)[row, 0]
                spot = (k * BLOCK + u) * ROW
                prod[spot:spot + ROW, :] = dtab[pl.ds(near, ROW), :] * dtab[pl.ds(far, ROW), :]
            one, two, three = (prod[pl.ds(k * BLOCK * ROW + c, BLOCK, stride=ROW), :] for c in range(3))
            sent[d, pl.ds(pl.multiple_of((s * 2 + k) * BLOCK, BLOCK), BLOCK), :] = ((one + two + three) * mine).astype(BF16)

    def sens_copy(s, d):
        axis, lo, hi = SUBS[s]
        where = pl.ds(lo * BLOCK, (hi - lo) * BLOCK)
        return pltpu.make_async_remote_copy(
            src_ref=sent.at[d, where, :], dst_ref=came.at[4 - d, where, :],
            send_sem=sens_send.at[s, d], recv_sem=sens_recv.at[s, 4 - d],
            device_id=at(**{axis: d}), device_id_type=MESH)

    def share(s, i=0, j=0):
        first, second = (where_am_i[axis] for axis in PLANE[SUBS[s][0]])
        return lax.rem(first + i, 4) * 4 + lax.rem(second + j, 4)

    def part_copy(s, d):
        axis, lo, hi = SUBS[s]
        first, second = PLANE[axis]
        i, j = deltas[d]
        where = pl.ds(lo * BLOCK, (hi - lo) * BLOCK)
        return pltpu.make_async_remote_copy(
            src_ref=part.at[share(s, i, j), :, where], dst_ref=got.at[back[d], :, where],
            send_sem=part_send.at[s, d], recv_sem=part_recv.at[s, back[d]],
            device_id=at(**{first: i, second: j}), device_id_type=MESH)

    def project(s):
        axis, lo, hi = SUBS[s]
        for d in range(1, 4):
            sens_copy(s, 4 - d).wait_recv()
        for m in range(lo, hi):
            rows = slice(m * BLOCK, (m + 1) * BLOCK)
            sens = jnp.concatenate([sent[0, rows, :]] + [came[d, rows, :] for d in range(1, 4)], axis=1)
            proj = lax.dot_general(bas_t["yxz".index(axis)], sens, (((1,), (1,)), ((), ())), preferred_element_type=F32)
            part[:, :, rows] = proj.astype(BF16).reshape(CHIPS, BASIS // CHIPS, BLOCK)
        for d in range(len(deltas)):
            part_copy(s, d).start()

    def pair_copy(s):
        _, lo, hi = SUBS[s]
        half = (hi - lo) // 2
        return pltpu.make_async_remote_copy(
            src_ref=sums.at[0, pl.ds(lo // 2, half)], dst_ref=both.at[pl.ds(lo + core * half, half)],
            send_sem=pair_send.at[s], recv_sem=pair_recv.at[s], device_id=sibling, device_id_type=MESH)

    ring = [(dc, dy) for dc in range(CORES) for dy in range(NY) if dc or dy]

    def ring_copy(s, dc, dy):
        _, lo, hi = SUBS[s]
        half = (hi - lo) // 2
        to = lax.rem(core + dc, CORES)
        return pltpu.make_async_remote_copy(
            src_ref=sums.at[to, pl.ds(lo // 2, half)], dst_ref=packed.at[pl.ds(lo * 4 + (y * CORES + core) * half, half)],
            send_sem=ring_send.at[s, dc, dy], recv_sem=ring_recv.at[s, dc, (NY - dy) % NY],
            device_id=(chip * CORES + to, on_ring(dy)), device_id_type=MESH)

    def add_up(s):
        axis, lo, hi = SUBS[s]
        where = slice(lo * BLOCK, hi * BLOCK)
        total = part[share(s), :, where].astype(F32)
        for d in range(len(deltas)):
            part_copy(s, back[d]).wait_recv()
            total = total + got[d, :, where].astype(F32)
        if axis == "y":
            for m in range(0, hi - lo, 2):
                for c in range(CORES):
                    sums[c, (lo + m) // 2] = jnp.concatenate([total[c * 8:(c + 1) * 8, k * BLOCK:(k + 1) * BLOCK] for k in (m, m + 1)], axis=0).astype(BF16)
            for dc, dy in ring:
                ring_copy(s, dc, dy).start()
            first = lo * 4 + (y * CORES + core) * ((hi - lo) // 2)
            for m in range((hi - lo) // 2):
                packed[first + m] = sums[core, lo // 2 + m]
            return
        for m in range(0, hi - lo, 2):
            pairs = [jnp.concatenate([total[c * 8:(c + 1) * 8, k * BLOCK:(k + 1) * BLOCK] for k in (m, m + 1)], axis=0).astype(BF16) for c in range(CORES)]
            kept = jnp.where(core == 0, pairs[0].astype(F32), pairs[1].astype(F32)).astype(BF16)
            sums[0, (lo + m) // 2] = jnp.where(core == 0, pairs[1].astype(F32), pairs[0].astype(F32)).astype(BF16)
            both[lo + core * ((hi - lo) // 2) + m // 2] = kept
        pair_copy(s).start()

    def out_copy(s, dy, source):
        axis, lo, hi = SUBS[s]
        return pltpu.make_async_remote_copy(
            src_ref=both.at[pl.ds(lo, hi - lo)], dst_ref=packed.at[pl.ds(lo * 4 + where_am_i[axis] * (hi - lo), hi - lo)],
            send_sem=out_send.at[s, dy], recv_sem=out_recv.at[s, source],
            device_id=(share(s) * CORES + core, on_ring(dy)), device_id_type=MESH)

    def send_out(s):
        axis, lo, hi = SUBS[s]
        pair_copy(s).wait_recv()
        for dy in range(1, NY):
            out_copy(s, dy, where_am_i[axis]).start()

        @pl.when(share(s) != chip)
        def _():
            out_copy(s, 0, where_am_i[axis]).start()

        @pl.when(share(s) == chip)
        def _():
            for m in range(hi - lo):
                packed[lo * 4 + where_am_i[axis] * (hi - lo) + m] = both[lo + m]

    def steps(n, _):
        part_now, d = lax.div(n, 4), lax.rem(n + 1, 4)
        candidates(part_now, d)
        for s in range(len(SUBS)):
            @pl.when((part_now == s) & (d != 0))
            def _():
                sens_copy(s, d).start()
        for s in range(len(SUBS) - LAG):
            @pl.when((part_now == s + LAG) & (d == 0))
            def _():
                project(s)
        return 0

    for copy in far:
        copy.wait()
    lax.fori_loop(0, 4 * len(SUBS), steps, 0)
    for s in range(len(SUBS) - LAG, len(SUBS)):
        project(s)
    hopping = [s for s, (axis, _, _) in enumerate(SUBS) if axis != "y"]
    for s in range(len(SUBS)):
        add_up(s)
        if s - 1 in hopping:
            send_out(s - 1)
    for s in range(len(SUBS)):
        for d in range(1, 4):
            sens_copy(s, d).wait_send()
        for d in range(len(deltas)):
            part_copy(s, d).wait_send()
    for copy in forwards:
        copy.wait_send()
    for h in range(2):
        @pl.when(h * CORES + core != y)
        def _():
            for piece in range(PARTS):
                pole_copy(h, piece).wait_send()
    for s, (axis, lo, hi) in enumerate(SUBS):
        if s not in hopping:
            for dc, dy in ring:
                ring_copy(s, dc, dy).wait_recv()
            continue
        for source in range(4):
            @pl.when((share(s) != chip) | (where_am_i[axis] != source))
            def _():
                out_copy(s, 1, source).wait_recv()

    for m in range(LIVE // BLOCK // 2):
        pair = packed[m].astype(F32)
        flat[2 * m] = pair[0:8, :]
        flat[2 * m + 1] = pair[8:16, :]
    first = jnp.int32(0)
    for g in range(1, NY):
        first = jnp.where(y == g, starts[g], first)
    whole, shift, limit = first // LANES, first % LANES, live[y]
    lane = lax.broadcasted_iota(I32, (8, LANES), 1)
    kept = LANES - shift
    turn = lax.rem(kept, LANES)
    turned = pltpu.roll(flat[whole], turn, 1)
    for b in range(Q_ROWS):
        then = pltpu.roll(flat[whole + b + 1], turn, 1)
        value = jnp.where(lane < kept, turned, then)
        out[:, b * LANES:(b + 1) * LANES] = jnp.where(lane + b * LANES < limit, value, 0.0)
        turned = then

    for s in range(len(SUBS)):
        if s not in hopping:
            for dc, dy in ring:
                ring_copy(s, dc, dy).wait_send()
            continue
        pair_copy(s).wait_send()
        for dy in range(1, NY):
            out_copy(s, dy, 0).wait_send()

        @pl.when(share(s) != chip)
        def _():
            out_copy(s, 0, 0).wait_send()


def on_device(pole_grads, endpoints, current, potential, live_counts, cell_weight, basis):
    poles = jnp.transpose(pole_grads, (1, 0, 2))
    endp = endpoints.T.reshape(2, DIP_G // LANES, LANES).transpose(1, 0, 2).reshape(2 * DIP_G // LANES, LANES)
    weight = cell_weight.reshape(2, LANES)
    vmem, dma = pltpu.VMEM, pltpu.SemaphoreType.DMA
    in_hbm = pl.BlockSpec(memory_space=pltpu.HBM)
    gains = pl.pallas_call(
        kernel,
        out_shape=jax.ShapeDtypeStruct((BASIS // CHIPS // CORES, Q_G), F32),
        in_specs=[in_hbm] * 4 + [pl.BlockSpec(memory_space=pltpu.SMEM)] + [in_hbm] * 2,
        out_specs=pl.BlockSpec(memory_space=vmem),
        scratch_shapes=[
            vmem((3, NY * POLES_G, LANES), BF16),
            vmem((NY * POLES_G * ROW, LANES), F32),
            vmem((NY * DIP_G * ROW, LANES), F32),
            vmem((MARGIN + NY * IDX_ROWS + MARGIN, LANES), I32),
            vmem((NY * 16 + 2 * LIST, LANES), I32),
            pltpu.SMEM((NY * 16 + 2 * LIST + 2, LANES), I32),
            vmem((2 * BLOCK * ROW, LANES), F32),
            vmem((NY, OWN_Q, LANES), BF16),
            vmem((NY, OWN_Q, LANES), BF16),
            vmem((CORES, 2, LANES), F32),
            vmem((NY, LANES, BASIS), BF16),
            vmem((BASIS, LANES), BF16),
            vmem((3, BASIS, 4 * LANES), BF16),
            vmem((CHIPS, BASIS // CHIPS, OWN_Q), BF16),
            vmem((CHIPS - 1, BASIS // CHIPS, OWN_Q), BF16),
            vmem((CORES, OWN_BLOCKS // 2, 16, BLOCK), BF16),
            vmem((OWN_BLOCKS, 16, BLOCK), BF16),
            vmem((LIVE // BLOCK // 2, 16, BLOCK), BF16),
            vmem((LIVE // BLOCK + Q_ROWS + 1, 8, BLOCK), F32),
            dma((6,)),
            dma((2, PARTS)), dma((NY, PARTS // CORES)), dma((NY, PARTS // CORES)), dma((NY, PARTS // CORES)), dma,
            dma((NY, 3)), dma((NY, 3)), dma,
            dma((3,)), dma((3,)),
            dma((3, 4)), dma((3, 4)),
            dma((len(SUBS), 4)), dma((len(SUBS), 4)),
            dma((len(SUBS), CHIPS - 1)), dma((len(SUBS), CHIPS - 1)),
            dma((len(SUBS),)), dma((len(SUBS),)),
            dma((len(SUBS), NY)), dma((len(SUBS), NY)),
            dma((len(SUBS), CORES, NY)), dma((len(SUBS), CORES, NY)),
        ],
        compiler_params=pltpu.CompilerParams(collective_id=0, has_side_effects=True, vmem_limit_bytes=60 * 2**20),
    )(poles, endp, current.reshape(Q_G // LANES, LANES), potential.reshape(Q_G // LANES, LANES), live_counts, weight, basis)
    return gains.astype(BF16)


def solution(mesh):
    placed = (
        P("holes", None, "cells"),
        P("holes", None),
        P("holes"),
        P("holes"),
        P(),
        P("cells"),
        P("cells", None),
    )
    return jax.shard_map(
        on_device, mesh=mesh, in_specs=placed, out_specs=P("cells", "holes"), check_vma=False
    )
```

```python
import functools

import jax
import jax.numpy as jnp
from jax import lax
from jax.experimental import pallas as pl
from jax.experimental.pallas import tpu as pltpu
from jax.sharding import PartitionSpec as P

F32, BF16, I32 = jnp.float32, jnp.bfloat16, jnp.int32
MESH = pl.DeviceIdType.MESH

LANES = 128
NY, NX, NZ, CORES = 4, 4, 4, 2
CHIPS = NX * NZ
POLES_G, DIP_G, Q_G, BASIS = 1536, 1024, 4096, 256
PARTS = 8
PIECE = POLES_G // PARTS
ROW = 4
BLOCK = 128
LIVE = 10240
OWN_BLOCKS = LIVE // (NY * CORES * BLOCK)
OWN_Q = OWN_BLOCKS * BLOCK
SUBS = (("y", 0, 2), ("x", 2, 4), ("z", 4, 6), ("x", 6, 8), ("y", 8, 10))
LAG = 5
PLANE = {"y": ("x", "z"), "x": ("y", "z"), "z": ("x", "y")}
IDX_ROWS = 80
Q_ROWS = Q_G // LANES
LIST = LIVE // LANES
MARGIN = 88


def kernel(poles, endp, cur, pot, live, weight, basis, out,
           landed, ptab, dtab, all_idx, lists, idx, prod, sent, came, wts, bas, bas_own, bas_t, part, got, sums, both, packed, flat,
           in_sem, pole_send, pole_recv, fwd_send, fwd_recv, own_sem, idx_send, idx_recv, idx_sem,
           small_send, small_recv, bas_send, bas_recv, sens_send, sens_recv, part_send, part_recv, pair_send, pair_recv, out_send, out_recv, ring_send, ring_recv):
    cells, y = lax.axis_index("cells"), lax.axis_index("holes")
    core, chip = lax.rem(cells, CORES), lax.div(cells, CORES)
    x, z = lax.div(chip, NZ), lax.rem(chip, NZ)
    sibling = (chip * CORES + 1 - core, y)

    def on_ring(dy):
        return lax.rem(y + dy, NY)

    where_am_i = {"x": x, "y": y, "z": z}

    def at(core_there=core, **steps):
        there = {axis: lax.rem(here + steps.get(axis, 0), 4) for axis, here in where_am_i.items()}
        return (there["x"] * NZ + there["z"]) * CORES + core_there, there["y"]

    deltas = [(i, j) for i in range(4) for j in range(4) if i or j]
    back = [deltas.index(((4 - i) % 4, (4 - j) % 4)) for i, j in deltas]

    barrier = pltpu.get_barrier_semaphore()
    greeted = [at(1 - core, y=dy) for dy in range(NY)]
    greeted += [at(x=i, y=j, z=k) for i in range(NX) for j in range(NY) for k in range(NZ) if (i or j or k) and not (i and j and k)]
    for device in greeted:
        pl.semaphore_signal(barrier, inc=1, device_id=device, device_id_type=MESH)

    def idx_ends(n):
        src, rows, size = ((endp, 0, 16), (cur, 16, 32), (pot, 48, 32))[n]
        return src, all_idx.at[pl.ds(pl.multiple_of(MARGIN + y * IDX_ROWS + rows, 8), size), :]

    small_ends = [(weight, wts.at[core]), (basis.at[0:LANES, :], bas.at[core]), (basis.at[LANES:2 * LANES, :], bas.at[CORES + core])]
    ins = [pltpu.make_async_copy(*ends, in_sem.at[n]) for n, ends in enumerate([idx_ends(0), idx_ends(1), idx_ends(2)] + small_ends)]
    for copy in ins:
        copy.start()

    pl.semaphore_wait(barrier, len(greeted))

    idx_copies, small = [], []
    for dy in range(1, NY):
        for n in range(3):
            src, dst = idx_ends(n)
            idx_copies.append(pltpu.make_async_remote_copy(
                src_ref=src, dst_ref=dst, send_sem=idx_send.at[dy, n], recv_sem=idx_recv.at[dy, n],
                device_id=(cells, on_ring(dy)), device_id_type=MESH))
    for n, (src, dst) in enumerate(small_ends):
        small.append(pltpu.make_async_remote_copy(src_ref=src, dst_ref=dst, send_sem=small_send.at[n], recv_sem=small_recv.at[n],
                                                  device_id=sibling, device_id_type=MESH))
    for copy in idx_copies + small:
        copy.start()

    def rows_of(group, piece):
        return pl.ds(pl.multiple_of(group * POLES_G + piece * PIECE, PIECE), PIECE)

    def pole_copy(h, piece):
        dest = h * CORES + core
        dy = lax.rem(y - dest + NY, NY)
        return pltpu.make_async_remote_copy(
            src_ref=poles.at[:, pl.ds(piece * PIECE, PIECE), pl.ds(h * LANES, LANES)],
            dst_ref=landed.at[:, rows_of(y, piece), :],
            send_sem=pole_send.at[h, piece], recv_sem=pole_recv.at[dy, piece // CORES],
            device_id=(chip * CORES + piece % CORES, dest), device_id_type=MESH)

    def own_ends(h):
        return poles.at[:, :, pl.ds(h * LANES, LANES)], landed.at[:, pl.ds(pl.multiple_of(y * POLES_G, POLES_G), POLES_G), :]

    def own_local(h):
        return pltpu.make_async_copy(*own_ends(h), own_sem)

    def own_remote(h):
        src, dst = own_ends(h)
        return pltpu.make_async_remote_copy(src_ref=src, dst_ref=dst, send_sem=fwd_send.at[0, 0], recv_sem=fwd_recv.at[0, 0],
                                            device_id=sibling, device_id_type=MESH)

    for h in range(2):
        @pl.when(h * CORES + core != y)
        def _():
            for piece in range(PARTS):
                pole_copy(h, piece).start()

        @pl.when(h * CORES + core == y)
        def _():
            own_local(h).start()
            own_remote(h).start()

    for copy in ins + small:
        copy.wait()
    bas_own[...] = jnp.transpose(bas[y].astype(F32)).astype(BF16)
    far = []
    for n, axis in enumerate("yxz"):
        bas_t[n, :, 0:LANES] = bas_own[...]
        for d in range(1, 4):
            if axis == "y":
                bas_t[n, :, d * LANES:(d + 1) * LANES] = jnp.transpose(bas[on_ring(d)].astype(F32)).astype(BF16)
                continue
            far.append(pltpu.make_async_remote_copy(
                src_ref=bas_own, dst_ref=bas_t.at[n, :, pl.ds((4 - d) * LANES, LANES)], send_sem=bas_send.at[n, d], recv_sem=bas_recv.at[n, 4 - d],
                device_id=at(**{axis: d}), device_id_type=MESH))
            far[-1].start()
    for copy in idx_copies:
        copy.wait()
    starts = [0]
    for g in range(NY - 1):
        starts.append(starts[-1] + live[g])
    for g in range(NY):
        first = MARGIN + g * IDX_ROWS
        lists[g * 16:(g + 1) * 16, :] = all_idx[first:first + 16, :] * ROW
    lane = lax.broadcasted_iota(I32, (LIST, LANES), 1)
    place = lax.broadcasted_iota(I32, (LIST, LANES), 0) * LANES + lane
    for n, offset in enumerate((16, 48)):
        total = jnp.zeros((LIST, LANES), I32)
        for g in range(NY):
            whole, shift = starts[g] // LANES, starts[g] % LANES
            window = MARGIN + g * IDX_ROWS + offset - whole
            same = pltpu.roll(all_idx[pl.ds(window, LIST), :], shift, 1)
            before = pltpu.roll(all_idx[pl.ds(window - 1, LIST), :], shift, 1)
            values = jnp.where(lane >= shift, same, before)
            if n == 0:
                values = values + g * DIP_G
            since = place - starts[g]
            total = jnp.where((since >= 0) & (since < live[g]), values, total)
        lists[NY * 16 + n * LIST:NY * 16 + (n + 1) * LIST, :] = total * ROW
    to_smem = pltpu.make_async_copy(lists, idx.at[pl.ds(0, lists.shape[0]), :], idx_sem)
    to_smem.start()
    to_smem.wait()

    def spread(group, piece):
        at = group * POLES_G + piece * PIECE
        for k in range(3):
            block = landed[k, pl.ds(pl.multiple_of(at, PIECE), PIECE), :].astype(F32)
            ptab[pl.ds(at * ROW + k, PIECE, stride=ROW), :] = block

    def forward(dy, n):
        where = landed.at[:, rows_of(on_ring(dy), n * CORES + core), :]
        return pltpu.make_async_remote_copy(src_ref=where, dst_ref=where, send_sem=fwd_send.at[dy, n], recv_sem=fwd_recv.at[dy, n],
                                            device_id=sibling, device_id_type=MESH)

    for h in range(2):
        @pl.when(h * CORES + core == y)
        def _():
            own_local(h).wait()
            own_remote(h).wait_send()

    @pl.when(lax.rem(y, CORES) != core)
    def _():
        own_remote(0).wait_recv()
    for piece in range(PARTS):
        spread(y, piece)

    forwards = []

    def from_sibling(dy, n):
        forward_there = landed.at[:, rows_of(on_ring(dy), n * CORES + 1 - core), :]
        pltpu.make_async_remote_copy(src_ref=forward_there, dst_ref=forward_there, send_sem=fwd_send.at[dy, n], recv_sem=fwd_recv.at[dy, n],
                                     device_id=sibling, device_id_type=MESH).wait_recv()
        spread(on_ring(dy), n * CORES + 1 - core)

    for n in range(PARTS // CORES):
        for dy in (1, 3, 2):
            where = landed.at[:, rows_of(on_ring(dy), n * CORES + core), :]
            pltpu.make_async_remote_copy(src_ref=where, dst_ref=where, send_sem=fwd_send.at[dy, n], recv_sem=pole_recv.at[dy, n],
                                         device_id=sibling, device_id_type=MESH).wait_recv()
            forwards.append(forward(dy, n))
            forwards[-1].start()
            spread(on_ring(dy), n * CORES + core)
            if n:
                from_sibling(dy, n - 1)
    for dy in (1, 3, 2):
        from_sibling(dy, PARTS // CORES - 1)

    def column(u, down):
        return idx.at[pl.ds(down, idx.shape[0] - LIST - 2), pl.ds(u, 1)]

    def dipoles(b, _):
        for k in range(2):
            for u in range(BLOCK):
                plus, minus = column(u, 2 * k)[b * 4, 0], column(u, 2 * k + 1)[b * 4, 0]
                spot = (k * BLOCK + u) * ROW
                prod[spot:spot + ROW, :] = ptab[pl.ds(plus, ROW), :] - ptab[pl.ds(minus, ROW), :]
            done = prod[k * BLOCK * ROW:(k + 1) * BLOCK * ROW, :].astype(BF16).astype(F32)
            dtab[pl.ds(pl.multiple_of((b * 2 + k) * (BLOCK * ROW), BLOCK * ROW), BLOCK * ROW), :] = done
        return 0

    lax.fori_loop(0, NY * DIP_G // BLOCK // 2, dipoles, 0)

    mine = wts[lax.rem(y, CORES), pl.ds(lax.div(y, CORES), 1), :]

    def candidates(s, d):
        there = jnp.int32(0)
        for n, (axis, _, _) in enumerate(SUBS):
            there = jnp.where(s == n, where_am_i[axis], there)
        row = NY * 16 + s * 16 + (lax.rem(there + d, 4) * CORES + core) * 2
        for k in range(2):
            for u in range(BLOCK):
                near, far = column(u, k)[row, 0], column(u, k + LIST)[row, 0]
                spot = (k * BLOCK + u) * ROW
                prod[spot:spot + ROW, :] = dtab[pl.ds(near, ROW), :] * dtab[pl.ds(far, ROW), :]
            one, two, three = (prod[pl.ds(k * BLOCK * ROW + c, BLOCK, stride=ROW), :] for c in range(3))
            sent[d, pl.ds(pl.multiple_of((s * 2 + k) * BLOCK, BLOCK), BLOCK), :] = ((one + two + three) * mine).astype(BF16)

    def sens_copy(s, d):
        axis, lo, hi = SUBS[s]
        where = pl.ds(lo * BLOCK, (hi - lo) * BLOCK)
        return pltpu.make_async_remote_copy(
            src_ref=sent.at[d, where, :], dst_ref=came.at[4 - d, where, :],
            send_sem=sens_send.at[s, d], recv_sem=sens_recv.at[s, 4 - d],
            device_id=at(**{axis: d}), device_id_type=MESH)

    def share(s, i=0, j=0):
        first, second = (where_am_i[axis] for axis in PLANE[SUBS[s][0]])
        return lax.rem(first + i, 4) * 4 + lax.rem(second + j, 4)

    def part_copy(s, d):
        axis, lo, hi = SUBS[s]
        first, second = PLANE[axis]
        i, j = deltas[d]
        where = pl.ds(lo * BLOCK, (hi - lo) * BLOCK)
        return pltpu.make_async_remote_copy(
            src_ref=part.at[share(s, i, j), :, where], dst_ref=got.at[back[d], :, where],
            send_sem=part_send.at[s, d], recv_sem=part_recv.at[s, back[d]],
            device_id=at(**{first: i, second: j}), device_id_type=MESH)

    def project(s):
        axis, lo, hi = SUBS[s]
        for d in range(1, 4):
            sens_copy(s, 4 - d).wait_recv()
        for m in range(lo, hi):
            rows = slice(m * BLOCK, (m + 1) * BLOCK)
            sens = jnp.concatenate([sent[0, rows, :]] + [came[d, rows, :] for d in range(1, 4)], axis=1)
            proj = lax.dot_general(bas_t["yxz".index(axis)], sens, (((1,), (1,)), ((), ())), preferred_element_type=F32)
            part[:, :, rows] = proj.astype(BF16).reshape(CHIPS, BASIS // CHIPS, BLOCK)
        for d in range(len(deltas)):
            part_copy(s, d).start()

    def pair_copy(s):
        _, lo, hi = SUBS[s]
        half = (hi - lo) // 2
        return pltpu.make_async_remote_copy(
            src_ref=sums.at[0, pl.ds(lo // 2, half)], dst_ref=both.at[pl.ds(lo + core * half, half)],
            send_sem=pair_send.at[s], recv_sem=pair_recv.at[s], device_id=sibling, device_id_type=MESH)

    ring = [(dc, dy) for dc in range(CORES) for dy in range(NY) if dc or dy]

    def ring_copy(s, dc, dy):
        _, lo, hi = SUBS[s]
        half = (hi - lo) // 2
        to = lax.rem(core + dc, CORES)
        return pltpu.make_async_remote_copy(
            src_ref=sums.at[to, pl.ds(lo // 2, half)], dst_ref=packed.at[pl.ds(lo * 4 + (y * CORES + core) * half, half)],
            send_sem=ring_send.at[s, dc, dy], recv_sem=ring_recv.at[s, dc, (NY - dy) % NY],
            device_id=(chip * CORES + to, on_ring(dy)), device_id_type=MESH)

    def add_up(s):
        axis, lo, hi = SUBS[s]
        where = slice(lo * BLOCK, hi * BLOCK)
        total = part[share(s), :, where].astype(F32)
        for d in range(len(deltas)):
            part_copy(s, back[d]).wait_recv()
            total = total + got[d, :, where].astype(F32)
        if axis == "y":
            for m in range(0, hi - lo, 2):
                for c in range(CORES):
                    sums[c, (lo + m) // 2] = jnp.concatenate([total[c * 8:(c + 1) * 8, k * BLOCK:(k + 1) * BLOCK] for k in (m, m + 1)], axis=0).astype(BF16)
            for dc, dy in ring:
                ring_copy(s, dc, dy).start()
            first = lo * 4 + (y * CORES + core) * ((hi - lo) // 2)
            for m in range((hi - lo) // 2):
                packed[first + m] = sums[core, lo // 2 + m]
            return
        for m in range(0, hi - lo, 2):
            pairs = [jnp.concatenate([total[c * 8:(c + 1) * 8, k * BLOCK:(k + 1) * BLOCK] for k in (m, m + 1)], axis=0).astype(BF16) for c in range(CORES)]
            kept = jnp.where(core == 0, pairs[0].astype(F32), pairs[1].astype(F32)).astype(BF16)
            sums[0, (lo + m) // 2] = jnp.where(core == 0, pairs[1].astype(F32), pairs[0].astype(F32)).astype(BF16)
            both[lo + core * ((hi - lo) // 2) + m // 2] = kept
        pair_copy(s).start()

    def out_copy(s, dy, source):
        axis, lo, hi = SUBS[s]
        return pltpu.make_async_remote_copy(
            src_ref=both.at[pl.ds(lo, hi - lo)], dst_ref=packed.at[pl.ds(lo * 4 + where_am_i[axis] * (hi - lo), hi - lo)],
            send_sem=out_send.at[s, dy], recv_sem=out_recv.at[s, source],
            device_id=(share(s) * CORES + core, on_ring(dy)), device_id_type=MESH)

    def send_out(s):
        axis, lo, hi = SUBS[s]
        pair_copy(s).wait_recv()
        for dy in range(1, NY):
            out_copy(s, dy, where_am_i[axis]).start()

        @pl.when(share(s) != chip)
        def _():
            out_copy(s, 0, where_am_i[axis]).start()

        @pl.when(share(s) == chip)
        def _():
            for m in range(hi - lo):
                packed[lo * 4 + where_am_i[axis] * (hi - lo) + m] = both[lo + m]

    def steps(n, _):
        part_now, d = lax.div(n, 4), lax.rem(n + 1, 4)
        candidates(part_now, d)
        for s in range(len(SUBS)):
            @pl.when((part_now == s) & (d != 0))
            def _():
                sens_copy(s, d).start()
        for s in range(len(SUBS) - LAG):
            @pl.when((part_now == s + LAG) & (d == 0))
            def _():
                project(s)
        return 0

    for copy in far:
        copy.wait()
    lax.fori_loop(0, 4 * len(SUBS), steps, 0)
    for s in range(len(SUBS) - LAG, len(SUBS)):
        project(s)
    hopping = [s for s, (axis, _, _) in enumerate(SUBS) if axis != "y"]
    for s in range(len(SUBS)):
        add_up(s)
        if s - 1 in hopping:
            send_out(s - 1)
    for s in range(len(SUBS)):
        for d in range(1, 4):
            sens_copy(s, d).wait_send()
        for d in range(len(deltas)):
            part_copy(s, d).wait_send()
    for copy in forwards:
        copy.wait_send()
    for h in range(2):
        @pl.when(h * CORES + core != y)
        def _():
            for piece in range(PARTS):
                pole_copy(h, piece).wait_send()
    for s, (axis, lo, hi) in enumerate(SUBS):
        if s not in hopping:
            for dc, dy in ring:
                ring_copy(s, dc, dy).wait_recv()
            continue
        for source in range(4):
            @pl.when((share(s) != chip) | (where_am_i[axis] != source))
            def _():
                out_copy(s, 1, source).wait_recv()

    for m in range(LIVE // BLOCK // 2):
        pair = packed[m].astype(F32)
        flat[2 * m] = pair[0:8, :]
        flat[2 * m + 1] = pair[8:16, :]
    first = jnp.int32(0)
    for g in range(1, NY):
        first = jnp.where(y == g, starts[g], first)
    whole, shift, limit = first // LANES, first % LANES, live[y]
    lane = lax.broadcasted_iota(I32, (8, LANES), 1)
    kept = LANES - shift
    turn = lax.rem(kept, LANES)
    turned = pltpu.roll(flat[whole], turn, 1)
    for b in range(Q_ROWS):
        then = pltpu.roll(flat[whole + b + 1], turn, 1)
        value = jnp.where(lane < kept, turned, then)
        out[:, b * LANES:(b + 1) * LANES] = jnp.where(lane + b * LANES < limit, value, 0.0)
        turned = then

    for s in range(len(SUBS)):
        if s not in hopping:
            for dc, dy in ring:
                ring_copy(s, dc, dy).wait_send()
            continue
        pair_copy(s).wait_send()
        for dy in range(1, NY):
            out_copy(s, dy, 0).wait_send()

        @pl.when(share(s) != chip)
        def _():
            out_copy(s, 0, 0).wait_send()


def on_device(pole_grads, endpoints, current, potential, live_counts, cell_weight, basis):
    poles = jnp.transpose(pole_grads, (1, 0, 2))
    endp = endpoints.T.reshape(2, DIP_G // LANES, LANES).transpose(1, 0, 2).reshape(2 * DIP_G // LANES, LANES)
    weight = cell_weight.reshape(2, LANES)
    vmem, dma = pltpu.VMEM, pltpu.SemaphoreType.DMA
    in_hbm = pl.BlockSpec(memory_space=pltpu.HBM)
    gains = pl.pallas_call(
        kernel,
        out_shape=jax.ShapeDtypeStruct((BASIS // CHIPS // CORES, Q_G), F32),
        in_specs=[in_hbm] * 4 + [pl.BlockSpec(memory_space=pltpu.SMEM)] + [in_hbm] * 2,
        out_specs=pl.BlockSpec(memory_space=vmem),
        scratch_shapes=[
            vmem((3, NY * POLES_G, LANES), BF16),
            vmem((NY * POLES_G * ROW, LANES), F32),
            vmem((NY * DIP_G * ROW, LANES), F32),
            vmem((MARGIN + NY * IDX_ROWS + MARGIN, LANES), I32),
            vmem((NY * 16 + 2 * LIST, LANES), I32),
            pltpu.SMEM((NY * 16 + 2 * LIST + 2, LANES), I32),
            vmem((2 * BLOCK * ROW, LANES), F32),
            vmem((NY, OWN_Q, LANES), BF16),
            vmem((NY, OWN_Q, LANES), BF16),
            vmem((CORES, 2, LANES), F32),
            vmem((NY, LANES, BASIS), BF16),
            vmem((BASIS, LANES), BF16),
            vmem((3, BASIS, 4 * LANES), BF16),
            vmem((CHIPS, BASIS // CHIPS, OWN_Q), BF16),
            vmem((CHIPS - 1, BASIS // CHIPS, OWN_Q), BF16),
            vmem((CORES, OWN_BLOCKS // 2, 16, BLOCK), BF16),
            vmem((OWN_BLOCKS, 16, BLOCK), BF16),
            vmem((LIVE // BLOCK // 2, 16, BLOCK), BF16),
            vmem((LIVE // BLOCK + Q_ROWS + 1, 8, BLOCK), F32),
            dma((6,)),
            dma((2, PARTS)), dma((NY, PARTS // CORES)), dma((NY, PARTS // CORES)), dma((NY, PARTS // CORES)), dma,
            dma((NY, 3)), dma((NY, 3)), dma,
            dma((3,)), dma((3,)),
            dma((3, 4)), dma((3, 4)),
            dma((len(SUBS), 4)), dma((len(SUBS), 4)),
            dma((len(SUBS), CHIPS - 1)), dma((len(SUBS), CHIPS - 1)),
            dma((len(SUBS),)), dma((len(SUBS),)),
            dma((len(SUBS), NY)), dma((len(SUBS), NY)),
            dma((len(SUBS), CORES, NY)), dma((len(SUBS), CORES, NY)),
        ],
        compiler_params=pltpu.CompilerParams(collective_id=0, has_side_effects=True, vmem_limit_bytes=60 * 2**20),
    )(poles, endp, current.reshape(Q_G // LANES, LANES), potential.reshape(Q_G // LANES, LANES), live_counts, weight, basis)
    return gains.astype(BF16)


def solution(mesh):
    placed = (
        P("holes", None, "cells"),
        P("holes", None),
        P("holes"),
        P("holes"),
        P(),
        P("cells"),
        P("cells", None),
    )
    return jax.shard_map(
        on_device, mesh=mesh, in_specs=placed, out_specs=P("cells", "holes"), check_vma=False
    )
```
